32 devices in a mesh: dp: 4 (over z), table: 8 (over y, x, core).
Axes of the slice: x: 2, y: 2, z: 4, core: 2. Of those that a mesh axis runs over, the one named last changes fastest.
Arguments:
- core_ids: int32 [4096, 8, 3, 2], P(('dp', 'table')), may hold values from 0 to 249
- bag_lengths: int32 [4096, 8], P(('dp', 'table')), may hold values from 1 to 2
- first_core: bfloat16 [8, 250, 512], P('table'), may hold values from -6 to 6
- middle_core: bfloat16 [8, 250, 64, 128], P('table'), may hold values from -0.75 to 0.75
- last_core: bfloat16 [8, 250, 512], P('table'), may hold values from -0.75 to 0.75
- grad_hidden: bfloat16 [4096, 1024], P(('dp', 'table')), may hold values from -0.1875 to 0.1875
Outputs:
- pooled: bfloat16 [4096, 1024], P(('dp', 'table'))
- weight_grad: float32 [1024, 1024], P('table', 'dp')
The draws below stay inside these ranges and needn't reach their ends.
Inputs may be any that keep to these rules, and one draw needn't show every extreme that they name: `core_ids`: slots j >= bag_lengths[n, t] hold ids that are not used.
All inputs are finite; a program needn't handle non-finite values.
Results may differ from the reference program's by a relative error of at most 0.005.
Values may be sent and summed in bfloat16 or wider, within the bound.
A program may use at most 128 MiB of HBM per device.

```python
import jax
import jax.numpy as jnp
from jax import lax

D1 = 8
D2 = 2
D3 = 8
RANK = 64
NCORE = 250
HID = 1024
BAG = 2
TABLES = 8
BATCH = 4096


def set_ends(entries, rng, least, high):
    dims = entries.shape
    spot = [jax.random.randint(jax.random.fold_in(rng, axis), (), 0, dims[axis]) for axis in range(len(dims))]
    entries = entries.at[tuple(spot)].set(least)
    longest = dims.index(max(dims))
    spot[longest] = (spot[longest] + 1) % dims[longest]
    return entries.at[tuple(spot)].set(high)


def raised(entries, key, source, target, parts, factor):
    owner, partner = [(jnp.arange(entries.shape[dim]) // (entries.shape[dim] // parts)).reshape([-1 if axis == dim else 1 for axis in range(entries.ndim)]) for dim in (source, target)]
    chosen = jax.random.permutation(key, parts)[partner]
    strong = (owner == chosen) | (owner == (partner + parts // 2) % parts)
    return jnp.where(strong, factor * entries, entries)


def level_of(key, extent, pieces, smallest, largest):
    loudness = 1.0
    for dim, blocks in pieces:
        draws = jax.random.uniform(jax.random.fold_in(jax.random.fold_in(key, 6), dim), (blocks,), jnp.float32, smallest / len(pieces), largest / len(pieces))
        loudness = loudness * jnp.repeat(jnp.exp(draws), extent[dim] // blocks).reshape((-1,) + (1,) * (len(extent) - 1 - dim))
    return loudness


def centred(own_key, dims, width, limit, pieces=(), kind=jnp.bfloat16):
    array = jax.random.normal(own_key, dims, jnp.float32) * width
    if len(pieces) > 0:
        array = level_of(own_key, dims, pieces, -0.22, 0.18) * array
    return jnp.clip(array, min=-limit, max=limit).astype(kind)


def heavy_noise(key, shape, scale, limit, pieces, heavy, kind=jnp.bfloat16):
    entries = scale * jax.random.normal(key, shape, jnp.float32)
    if pieces:
        entries = entries * level_of(key, shape, pieces, -0.22, 0.18)
    return jnp.clip(raised(entries, jax.random.fold_in(key, 3), *heavy), -limit, limit).astype(kind)


def setup_inputs(seed: int = 0) -> dict:
    streams_of = jax.random.split(jax.random.key(seed), 7)
    return {
        "core_ids": set_ends(jax.random.randint(streams_of[0], (BATCH, TABLES, 3, BAG), 0, NCORE), jax.random.fold_in(streams_of[0], 1), 0, NCORE - 1).astype(jnp.int32),
        "bag_lengths": set_ends(jax.random.randint(streams_of[1], (BATCH, TABLES), 1, BAG + 1), jax.random.fold_in(streams_of[1], 1), 1, BAG).astype(jnp.int32),
        "first_core": centred(streams_of[2], (TABLES, NCORE, D1 * RANK), 1.0, 6.0, ((0, 8),)),
        "middle_core": centred(streams_of[3], (TABLES, NCORE, RANK, D2 * RANK), RANK ** -0.5, 0.75, ((0, 8),)),
        "last_core": centred(streams_of[4], (TABLES, NCORE, RANK * D3), RANK ** -0.5, 0.75, ((0, 8),)),
        "grad_hidden": heavy_noise(streams_of[5], (BATCH, HID), BATCH ** -0.5, 0.1875, ((0, 32),), (0, 1, 32, 2.75)),
    }


def build_rows(wanted, counts, first, middle, last):
    block = wanted.shape[0]
    head = jnp.take(first, wanted[:, 0, :], axis=0).astype(jnp.float32).reshape(block, BAG, D1, RANK)
    centre = jnp.take(middle, wanted[:, 1, :], axis=0).astype(jnp.float32)
    prefix = jnp.einsum('njar,njrs->njas', head, centre).astype(jnp.bfloat16)
    prefix = lax.optimization_barrier(prefix).astype(jnp.float32).reshape(block, BAG, D1 * D2, RANK)
    tail = jnp.take(last, wanted[:, 2, :], axis=0).astype(jnp.float32).reshape(block, BAG, RANK, D3)
    rows = jnp.einsum('njps,njsc->njpc', prefix, tail).reshape(block, BAG, D1 * D2 * D3)
    live = (jnp.arange(BAG, dtype=jnp.int32)[None, :] < counts[:, None]).astype(jnp.float32)
    return jnp.sum(rows * live[:, :, None], axis=1).astype(jnp.bfloat16)


def reference(core_ids, bag_lengths, first_core, middle_core, last_core, grad_hidden):
    block = min(BATCH, 1024)
    steps_count = BATCH // block

    def one_table(items):
        first, middle, last, wanted, counts = items
        wanted = wanted.reshape(steps_count, block, 3, BAG)
        counts = counts.reshape(steps_count, block)
        out = lax.map(lambda pair: build_rows(pair[0], pair[1], first, middle, last), (wanted, counts))
        return out.reshape(BATCH, D1 * D2 * D3)

    per_table = lax.map(one_table, (first_core, middle_core, last_core,
                                    jnp.transpose(core_ids, (1, 0, 2, 3)), jnp.transpose(bag_lengths)))
    pooled = jnp.transpose(per_table, (1, 0, 2)).reshape(BATCH, TABLES * D1 * D2 * D3)
    weight_grad = jnp.dot(pooled.T, grad_hidden, preferred_element_type=jnp.float32)
    return pooled, weight_grad
```

```python
import functools

import jax
import jax.numpy as jnp
from jax import lax
from jax.experimental import pallas as pl
from jax.experimental.pallas import tpu as pltpu
from jax.sharding import PartitionSpec as P

D1 = 8
D2 = 2
D3 = 8
RANK = 64
BAG = 2
LANES = 128
WIDTH = D1 * D2 * D3
SPAN = D1 * LANES
PAD = 256
UNROLL = 2
MESH = pl.DeviceIdType.MESH
F32 = jnp.float32
BF16 = jnp.bfloat16


def iota(shape, dim):
    return lax.broadcasted_iota(jnp.int32, shape, dim)


def spread_tables(first, last, firstx, lastx):
    ncore, wide = first.shape
    firstx[...] = jnp.zeros_like(firstx)
    lastx[...] = jnp.zeros_like(lastx)
    row = iota((wide, LANES), 0)
    lane = lax.rem(iota((wide, LANES), 1), RANK)
    for a in range(D1):
        span = slice(a * LANES, (a + 1) * LANES)
        pick = (row == a * RANK + lane).astype(F32).astype(BF16)
        firstx[0:ncore, span] = jnp.dot(first[...], pick, preferred_element_type=F32).astype(BF16)
        pick = (row == lane * D3 + a).astype(F32).astype(BF16)
        lastx[0:ncore, span] = jnp.dot(last[...], pick, preferred_element_type=F32).astype(BF16)


def gather_ends(tile, firstx, lastx, heads, tails):
    block = tile.shape[1]
    columns = jnp.transpose(tile)
    slices = iota((block, PAD), 1)
    for j in range(BAG):
        live = columns[:, 6:7] > j
        p = jnp.where(live, columns[:, j : j + 1], -1)
        u = columns[:, 4 + j : 5 + j]
        hot = (p == slices).astype(F32).astype(BF16)
        heads[j] = jnp.dot(hot, firstx[...], preferred_element_type=F32)
        hot = (u == slices).astype(F32).astype(BF16)
        tails[j] = jnp.dot(hot, lastx[...], preferred_element_type=F32)


def lookups(smem, slot, middle, heads, tails, spread, block):
    row16, lane16 = iota((16, LANES), 0), iota((16, LANES), 1)
    half = lane16 // RANK
    masks = []
    for kt in range(4):
        keep = (lax.rem(row16, 8) == 2 * kt + half).astype(F32).astype(BF16)
        masks.append(jnp.concatenate([keep] * 4, axis=0))
    sides = []
    for b in range(D2):
        keep = (half == b).astype(F32).astype(BF16)
        sides.append(jnp.concatenate([keep] * 4, axis=0))
    diagonal = (iota((8, LANES), 0) == lax.rem(iota((8, LANES), 1), 8)).astype(F32)
    diagonal = jnp.concatenate([diagonal] * D1, axis=0)

    def step(g, carry):
        base = pl.multiple_of(g * 16, 16)
        parts = []
        for h in range(2):
            at = base + 8 * h
            rows = pl.ds(pl.multiple_of(at, 8), 8)
            total = None
            for j in range(BAG):
                head = jnp.concatenate(
                    [heads[j, rows, a * LANES : (a + 1) * LANES] for a in range(D1)], axis=0
                ).astype(BF16)
                head = jnp.concatenate([head * mask for mask in masks], axis=1)
                centre = jnp.concatenate(
                    [middle[smem[slot, 2 + j, at + i]] for i in range(8)], axis=0
                )
                prefix = jnp.dot(head, centre, preferred_element_type=F32).astype(BF16)
                tail = jnp.concatenate(
                    [tails[j, rows, c * LANES : (c + 1) * LANES] for c in range(D3)], axis=0
                ).astype(BF16)
                tail = jnp.concatenate([tail * side for side in sides], axis=0)
                out = lax.dot_general(
                    prefix, tail, (((1,), (1,)), ((), ())), preferred_element_type=F32
                )
                total = out if total is None else total + out
            parts.append(total * diagonal)
        for a in range(D1):
            both = jnp.concatenate([part[a * 8 : (a + 1) * 8] for part in parts], axis=0)
            spread[pl.ds(base, 16), a * LANES : (a + 1) * LANES] = both.astype(BF16)
        return carry

    lax.fori_loop(0, block // 16, step, 0, unroll=UNROLL)


def kernel(nd, nt, tiles, first, middle, last, grad, pooled, wg,
           ids, smem, mid, grads, rows, sib, firstx, lastx, heads, tails, spread, fold, part, partin,
           mid_sem, smem_sem, ids_ss, ids_rs, grad_ss, grad_rs, pool_ss, pool_rs, sib_ss, sib_rs,
           part_ss, part_rs):
    d, t = lax.axis_index("dp"), lax.axis_index("table")
    core = lax.rem(t, 2)
    pair = t - core
    other = pair + 1 - core
    block = grad.shape[0]
    half = grads.shape[2]
    cols = wg.shape[1]
    per = nd // 2

    load = pltpu.make_async_copy(middle, mid, mid_sem)
    load.start()
    pltpu.make_async_copy(tiles.at[t], smem.at[0], smem_sem.at[0]).start()

    barrier = pltpu.get_barrier_semaphore()
    for k in range(1, nt):
        pl.semaphore_signal(barrier, inc=1, device_id=(d, lax.rem(t + k, nt)), device_id_type=MESH)
    for k in range(1, nd):
        for e in range(2):
            pl.semaphore_signal(
                barrier, inc=1, device_id=(lax.rem(d + k, nd), pair + e), device_id_type=MESH
            )
    pl.semaphore_wait(barrier, nt - 1 + 2 * (nd - 1))

    def send_ids(k):
        peer = lax.rem(t + k, nt)
        return pltpu.make_async_remote_copy(
            tiles.at[peer], ids.at[t], ids_ss.at[k], ids_rs.at[k],
            device_id=(d, peer), device_id_type=MESH)

    def send_grad(k):
        peer = lax.rem(t + k, nt)
        mine = pl.ds(pl.multiple_of(lax.rem(peer, 2) * half, LANES), half)
        return pltpu.make_async_remote_copy(
            grad.at[:, mine], grads.at[t], grad_ss.at[k], grad_rs.at[k],
            device_id=(d, peer), device_id_type=MESH)

    def send_pooled(k):
        peer = lax.rem(t - k + nt, nt)
        return pltpu.make_async_remote_copy(
            rows.at[peer], pooled.at[:, pl.ds(pl.multiple_of(t * WIDTH, LANES), WIDTH)],
            pool_ss.at[k], pool_rs.at[k], device_id=(d, peer), device_id_type=MESH)

    def send_sib(k):
        peer = lax.rem(t - k + nt, nt)
        return pltpu.make_async_remote_copy(
            rows.at[peer], sib.at[peer], sib_ss.at[peer], sib_rs.at[peer],
            device_id=(d, other), device_id_type=MESH)

    for k in range(1, nt):
        send_ids(k).start()
    for k in range(1, nt):
        send_grad(k).start()
    ids[t] = tiles[t]
    grads[t] = grad[:, pl.ds(pl.multiple_of(core * half, LANES), half)]

    spread_tables(first, last, firstx, lastx)
    fold[...] = (iota(fold.shape, 0) // 8 == iota(fold.shape, 1)).astype(F32).astype(BF16)
    load.wait()

    def chunk(k, carry):
        s = lax.rem(t - k + nt, nt)
        slot = lax.rem(k, 2)
        pltpu.make_async_copy(ids.at[s], smem.at[slot], smem_sem.at[slot]).wait()

        @pl.when(k + 1 < nt)
        def _():
            after = lax.rem(t - k - 1 + nt, nt)
            pltpu.make_async_remote_copy(
                ids.at[after], ids.at[after], ids_ss.at[k + 1], ids_rs.at[k + 1],
                device_id=(d, other), device_id_type=MESH).wait_recv()
            pltpu.make_async_copy(ids.at[after], smem.at[1 - slot], smem_sem.at[1 - slot]).start()

        gather_ends(ids[s], firstx, lastx, heads, tails)
        lookups(smem, slot, mid, heads, tails, spread, block)
        done = jnp.dot(spread[...], fold[...], preferred_element_type=F32).astype(BF16)
        rows[s] = done
        send_sib(k).start()

        @pl.when(k > 0)
        def _():
            send_pooled(k).start()

        @pl.when(k == 0)
        def _():
            pooled[:, pl.ds(pl.multiple_of(t * WIDTH, LANES), WIDTH)] = done

        return carry

    lax.fori_loop(0, nt, chunk, 0)

    for k in range(1, nt):
        s = lax.rem(t - k + nt, nt)
        pltpu.make_async_remote_copy(
            grads.at[s], grads.at[s], grad_ss.at[k], grad_rs.at[k],
            device_id=(d, other), device_id_type=MESH).wait_recv()
    for s in range(nt):
        pltpu.make_async_remote_copy(
            sib.at[s], sib.at[s], sib_ss.at[s], sib_rs.at[s],
            device_id=(d, other), device_id_type=MESH).wait_recv()

    group = nt * block

    def partial(mine, q):
        left = rows if mine else sib
        return lax.dot_general(
            left[...].reshape(group, WIDTH), grads[:, :, q * cols : (q + 1) * cols].reshape(group, cols),
            (((0,), (0,)), ((), ())), preferred_element_type=F32).astype(BF16)

    def send_part(mine, q):
        target = core * per + q
        return pltpu.make_async_remote_copy(
            part.at[mine, q], partin.at[d], part_ss.at[mine, q], part_rs.at[d],
            device_id=(target, t if mine else other), device_id_type=MESH)

    for mine in (1, 0):
        for q in range(per):
            part[mine, q] = partial(mine, q)
            if mine:
                @pl.when(core * per + q != d)
                def _():
                    send_part(mine, q).start()

                @pl.when(core * per + q == d)
                def _():
                    partin[d] = part[mine, q]
            else:
                send_part(mine, q).start()

    for k in range(1, nt):
        send_ids(k).wait_send()
        send_grad(k).wait_send()
        send_pooled(k).wait_send()
        s = lax.rem(t + k, nt)
        pltpu.make_async_remote_copy(
            rows.at[s], pooled.at[:, pl.ds(pl.multiple_of(s * WIDTH, LANES), WIDTH)],
            pool_ss.at[k], pool_rs.at[k], device_id=(d, other), device_id_type=MESH).wait_recv()
    for k in range(nt):
        send_sib(k).wait_send()

    source = d // per
    for k in range(nd):
        @pl.when(jnp.logical_or(source != core, k != d))
        def _():
            pltpu.make_async_remote_copy(
                partin.at[k], partin.at[k], part_ss.at[0, 0], part_rs.at[k],
                device_id=(d, other), device_id_type=MESH).wait_recv()
    total = partin[0].astype(F32)
    for k in range(1, nd):
        total = total + partin[k].astype(F32)
    wg[...] = total
    for mine in (1, 0):
        for q in range(per):
            if mine:
                @pl.when(core * per + q != d)
                def _():
                    send_part(mine, q).wait_send()
            else:
                send_part(mine, q).wait_send()


def body(core_ids, bag_lengths, first_core, middle_core, last_core, grad_hidden):
    nd, nt = lax.axis_size("dp"), lax.axis_size("table")
    block, hidden = grad_hidden.shape
    ncore = middle_core.shape[1]
    tiles = jnp.concatenate(
        [
            jnp.transpose(core_ids, (1, 2, 3, 0)).reshape(nt, 3 * BAG, block),
            jnp.transpose(bag_lengths)[:, None, :],
            jnp.zeros((nt, 1, block), jnp.int32),
        ],
        axis=1,
    )
    cols = hidden // nd
    half = hidden // 2
    vmem = pl.BlockSpec(memory_space=pltpu.VMEM)
    dma = pltpu.SemaphoreType.DMA
    return pl.pallas_call(
        functools.partial(kernel, nd, nt),
        out_shape=(
            jax.ShapeDtypeStruct((block, nt * WIDTH), BF16),
            jax.ShapeDtypeStruct((WIDTH, cols), F32),
        ),
        in_specs=[vmem, vmem, pl.BlockSpec(memory_space=pl.ANY), vmem, vmem],
        out_specs=(vmem, vmem),
        scratch_shapes=[
            pltpu.VMEM((nt, 8, block), jnp.int32),
            pltpu.SMEM((2, 8, block), jnp.int32),
            pltpu.VMEM((ncore, RANK, D2 * RANK), BF16),
            pltpu.VMEM((nt, block, half), BF16),
            pltpu.VMEM((nt, block, WIDTH), BF16),
            pltpu.VMEM((nt, block, WIDTH), BF16),
            pltpu.VMEM((PAD, SPAN), BF16),
            pltpu.VMEM((PAD, SPAN), BF16),
            pltpu.VMEM((BAG, block, SPAN), F32),
            pltpu.VMEM((BAG, block, SPAN), F32),
            pltpu.VMEM((block, SPAN), BF16),
            pltpu.VMEM((SPAN, WIDTH), BF16),
            pltpu.VMEM((2, nd // 2, WIDTH, cols), BF16),
            pltpu.VMEM((nd, WIDTH, cols), BF16),
            dma, dma((2,)),
            dma((nt,)), dma((nt,)), dma((nt,)), dma((nt,)), dma((nt,)), dma((nt,)),
            dma((nt,)), dma((nt,)), dma((2, nd // 2)), dma((nd,)),
        ],
        compiler_params=pltpu.CompilerParams(
            collective_id=0, has_side_effects=True, vmem_limit_bytes=48 * 1024 * 1024
        ),
        cost_estimate=pl.CostEstimate(flops=2 * 10**9, bytes_accessed=6 * 10**6, transcendentals=0),
    )(tiles, first_core[0], middle_core[0], last_core[0], grad_hidden)


def solution(mesh):
    placed = (
        P(("dp", "table"), None, None, None),
        P(("dp", "table"), None),
        P("table", None, None),
        P("table", None, None, None),
        P("table", None, None),
        P(("dp", "table"), None),
    )
    return jax.shard_map(
        body,
        mesh=mesh,
        in_specs=placed,
        out_specs=(P(("dp", "table"), None), P("table", "dp")),
        check_vma=False,
    )
```

```python
import functools

import jax
import jax.numpy as jnp
from jax import lax
from jax.experimental import pallas as pl
from jax.experimental.pallas import tpu as pltpu
from jax.sharding import PartitionSpec as P

D1 = 8
D2 = 2
D3 = 8
RANK = 64
BAG = 2
LANES = 128
WIDTH = D1 * D2 * D3
SPAN = D1 * LANES
LAG = 2
MESH = pl.DeviceIdType.MESH
F32 = jnp.float32
BF16 = jnp.bfloat16


def iota(shape, dim):
    return lax.broadcasted_iota(jnp.int32, shape, dim)


def spread_tables(first, last, firstx, wide, lastx):
    ncore, length = first.shape
    row = iota((length, LANES), 0)
    lane = lax.rem(iota((length, LANES), 1), RANK)
    half = iota((ncore, LANES), 1) // RANK
    wide[0 : firstx.shape[0] * D1] = jnp.zeros((firstx.shape[0] * D1, LANES), F32)
    for a in range(D1):
        pick = (row == a * RANK + lane).astype(F32).astype(BF16)
        wide[pl.ds(a, ncore, stride=D1), :] = jnp.dot(first[...], pick, preferred_element_type=F32)
    firstx[...] = wide[0 : firstx.shape[0] * D1].reshape(firstx.shape)
    for c in range(D3):
        pick = (row == lane * D3 + c).astype(F32).astype(BF16)
        found = jnp.dot(last[...], pick, preferred_element_type=F32)
        for b in range(D2):
            wide[pl.ds(b * D3 + c, ncore, stride=D2 * D3), :] = jnp.where(half == b, found, 0.0)
    lastx[...] = wide[...].reshape(lastx.shape).astype(BF16)


def heads_of(smem, slot, firstx, middle, at):
    upper = (iota((8, LANES), 1) >= RANK).astype(F32)
    lower = 1.0 - upper
    zero = jnp.zeros((16, LANES), BF16)
    groups = []
    for g in range(2):
        lefts, rights = [], []
        for j in range(BAG):
            heads, centres = [], []
            for i in range(4):
                n = at + g * 4 + i
                heads.append(firstx[smem[slot, j, n]] * (upper if i % 2 else lower))
                centres.append(middle[smem[slot, 2 + j, n]])
            top = jnp.concatenate(heads[:2], axis=0).astype(BF16)
            low = jnp.concatenate(heads[2:], axis=0).astype(BF16)
            lefts.append(jnp.concatenate([top, zero], axis=1))
            lefts.append(jnp.concatenate([zero, low], axis=1))
            rights.append(jnp.concatenate(centres, axis=0))
        both = jnp.dot(jnp.concatenate(lefts, axis=0), jnp.concatenate(rights, axis=1),
                       preferred_element_type=F32)
        groups.append(jnp.concatenate(
            [both[j * 32 : (j + 1) * 32, j * LANES : (j + 1) * LANES] for j in range(BAG)], axis=1
        ).astype(BF16))
    return jnp.concatenate(groups, axis=0)


def tails_of(smem, slot, prefix, lastx, at):
    sides = []
    for j in range(BAG):
        tails = []
        for i in range(8):
            tails.append(lastx[smem[slot, 4 + j, at + i]])
        sides.append(jnp.concatenate(tails, axis=0))
    out = lax.dot_general(prefix, jnp.concatenate(sides, axis=1), (((1,), (1,)), ((), ())),
                          preferred_element_type=F32)
    owner = iota((8, LANES), 1) // 16
    total = out[0:8]
    for i in range(1, 8):
        total = jnp.where(owner == i, out[i * 8 : (i + 1) * 8], total)
    return total


def lookups(smem, slot, firstx, middle, lastx, found, block):
    prefixes = {}
    count = block // 8
    for g in range(count + LAG):
        if g < count:
            prefixes[g] = heads_of(smem, slot, firstx, middle, g * 8)
        if g >= LAG:
            h = g - LAG
            found[h * 8 : (h + 1) * 8, :] = tails_of(smem, slot, prefixes.pop(h), lastx, h * 8)


def unfold(found, ordered, block):
    count = block // 8
    values = found[...].astype(BF16)
    row, col = iota((LANES, SPAN), 0), iota((LANES, SPAN), 1)
    copies = jnp.logical_and(row // 16 == col // LANES, lax.rem(row, 16) == lax.rem(col, 16))
    copied = jnp.dot(values, copies.astype(F32).astype(BF16), preferred_element_type=F32)
    row, col = iota((block, LANES), 0), iota((block, LANES), 1)
    keep = (lax.rem(row, 8) == col // 16).astype(F32)
    kept = jnp.concatenate(
        [copied[:, i * LANES : (i + 1) * LANES] * keep for i in range(8)], axis=1).astype(BF16)
    add = (iota((count, block), 1) // 8 == iota((count, block), 0)).astype(F32).astype(BF16)
    sums = jnp.dot(add, kept, preferred_element_type=F32)
    for i in range(8):
        ordered[pl.ds(i, count, stride=8), :] = sums[:, i * LANES : (i + 1) * LANES]
    return ordered[...].astype(BF16)


def kernel(nd, nt, core_ids, lengths, first, middle, last, grad, pooled, wg,
           raw_ids, raw_lengths, tiles, ids, smem, mid, ends, grads, rows, sib, firstx, wide, lastx, found, ordered, part, partin,
           raw_sem, mid_sem, end_sem, own_sem, smem_sem, ids_ss, ids_rs, grad_ss, grad_rs, pool_ss, pool_rs, sib_ss, sib_rs,
           part_ss, part_rs):
    d, t = lax.axis_index("dp"), lax.axis_index("table")
    core = lax.rem(t, 2)
    pair = t - core
    other = pair + 1 - core
    block = grad.shape[0]
    ncore = middle.shape[0]
    half = grads.shape[2]
    cols = wg.shape[1]
    per = nd // 2

    load = pltpu.make_async_copy(middle, mid, mid_sem)
    loads = [pltpu.make_async_copy(ref, ends.at[k], end_sem.at[k]) for k, ref in enumerate((first, last))]
    raws = [pltpu.make_async_copy(core_ids, raw_ids, raw_sem.at[0]),
            pltpu.make_async_copy(lengths, raw_lengths, raw_sem.at[1])]
    for copy in raws + loads:
        copy.start()
    load.start()

    barrier = pltpu.get_barrier_semaphore()
    for k in range(1, nt):
        pl.semaphore_signal(barrier, inc=1, device_id=(d, lax.rem(t + k, nt)), device_id_type=MESH)
    for k in range(1, nd):
        for e in range(2):
            pl.semaphore_signal(
                barrier, inc=1, device_id=(lax.rem(d + k, nd), pair + e), device_id_type=MESH
            )
    own = pltpu.make_async_copy(
        grad.at[:, pl.ds(pl.multiple_of(core * half, LANES), half)], grads.at[t], own_sem)
    own.start()
    for copy in raws:
        copy.wait()
    slots = iota((BAG, block), 0)
    for k in range(nt):
        live = slots < raw_lengths[k : k + 1, :]
        tiles[k, 0:BAG] = jnp.where(live, raw_ids[k, 0], ncore)
        tiles[k, BAG : 2 * BAG] = raw_ids[k, 1]
        tiles[k, 2 * BAG : 3 * BAG] = raw_ids[k, 2]
        tiles[k, 3 * BAG :] = jnp.zeros((8 - 3 * BAG, block), jnp.int32)
    pltpu.make_async_copy(tiles.at[t], smem.at[0], smem_sem.at[0]).start()
    for copy in loads:
        copy.wait()
    spread_tables(ends.at[0], ends.at[1], firstx, wide, lastx)
    pl.semaphore_wait(barrier, nt - 1 + 2 * (nd - 1))

    def send_ids(k):
        peer = lax.rem(t + k, nt)
        return pltpu.make_async_remote_copy(
            tiles.at[peer], ids.at[t], ids_ss.at[k], ids_rs.at[k],
            device_id=(d, peer), device_id_type=MESH)

    def send_grad(k):
        peer = lax.rem(t + k, nt)
        mine = pl.ds(pl.multiple_of(lax.rem(peer, 2) * half, LANES), half)
        return pltpu.make_async_remote_copy(
            grad.at[:, mine], grads.at[t], grad_ss.at[k], grad_rs.at[k],
            device_id=(d, peer), device_id_type=MESH)

    def send_pooled(k):
        peer = lax.rem(t - k + nt, nt)
        return pltpu.make_async_remote_copy(
            rows.at[peer], pooled.at[:, pl.ds(pl.multiple_of(t * WIDTH, LANES), WIDTH)],
            pool_ss.at[k], pool_rs.at[k], device_id=(d, peer), device_id_type=MESH)

    def send_sib(k):
        peer = lax.rem(t - k + nt, nt)
        return pltpu.make_async_remote_copy(
            rows.at[peer], sib.at[peer], sib_ss.at[peer], sib_rs.at[peer],
            device_id=(d, other), device_id_type=MESH)

    for k in range(1, nt):
        send_ids(k).start()
    for k in range(1, nt):
        send_grad(k).start()
    load.wait()

    def chunk(k, carry):
        s = lax.rem(t - k + nt, nt)
        slot = lax.rem(k, 2)
        pltpu.make_async_copy(ids.at[s], smem.at[slot], smem_sem.at[slot]).wait()

        @pl.when(k + 1 < nt)
        def _():
            after = lax.rem(t - k - 1 + nt, nt)
            pltpu.make_async_remote_copy(
                ids.at[after], ids.at[after], ids_ss.at[k + 1], ids_rs.at[k + 1],
                device_id=(d, other), device_id_type=MESH).wait_recv()
            pltpu.make_async_copy(ids.at[after], smem.at[1 - slot], smem_sem.at[1 - slot]).start()

        lookups(smem, slot, firstx, mid, lastx, found, block)
        done = unfold(found, ordered, block)
        rows[s] = done
        send_sib(k).start()

        @pl.when(k > 0)
        def _():
            send_pooled(k).start()

        @pl.when(k == 0)
        def _():
            pooled[:, pl.ds(pl.multiple_of(t * WIDTH, LANES), WIDTH)] = done

        return carry

    lax.fori_loop(0, nt, chunk, 0)
    own.wait()

    for k in range(1, nt):
        s = lax.rem(t - k + nt, nt)
        pltpu.make_async_remote_copy(
            grads.at[s], grads.at[s], grad_ss.at[k], grad_rs.at[k],
            device_id=(d, other), device_id_type=MESH).wait_recv()
    for s in range(nt):
        pltpu.make_async_remote_copy(
            sib.at[s], sib.at[s], sib_ss.at[s], sib_rs.at[s],
            device_id=(d, other), device_id_type=MESH).wait_recv()

    group = nt * block

    def partial(mine):
        left = rows if mine else sib
        return lax.dot_general(
            left[...].reshape(group, WIDTH), grads[...].reshape(group, half),
            (((0,), (0,)), ((), ())), preferred_element_type=F32).astype(BF16)

    def send_part(mine, q):
        target = core * per + q
        return pltpu.make_async_remote_copy(
            part.at[mine, q], partin.at[d], part_ss.at[mine, q], part_rs.at[d],
            device_id=(target, t if mine else other), device_id_type=MESH)

    for mine in (1, 0):
        whole = partial(mine)
        for q in range(per):
            part[mine, q] = whole[:, q * cols : (q + 1) * cols]
            if mine:
                @pl.when(core * per + q != d)
                def _():
                    send_part(mine, q).start()

                @pl.when(core * per + q == d)
                def _():
                    partin[d] = part[mine, q]
            else:
                send_part(mine, q).start()

    for k in range(1, nt):
        send_ids(k).wait_send()
        send_grad(k).wait_send()
        send_pooled(k).wait_send()
        s = lax.rem(t + k, nt)
        pltpu.make_async_remote_copy(
            rows.at[s], pooled.at[:, pl.ds(pl.multiple_of(s * WIDTH, LANES), WIDTH)],
            pool_ss.at[k], pool_rs.at[k], device_id=(d, other), device_id_type=MESH).wait_recv()
    for k in range(nt):
        send_sib(k).wait_send()

    source = d // per
    for k in range(nd):
        @pl.when(jnp.logical_or(source != core, k != d))
        def _():
            pltpu.make_async_remote_copy(
                partin.at[k], partin.at[k], part_ss.at[0, 0], part_rs.at[k],
                device_id=(d, other), device_id_type=MESH).wait_recv()
    total = partin[0].astype(F32)
    for k in range(1, nd):
        total = total + partin[k].astype(F32)
    wg[...] = total
    for mine in (1, 0):
        for q in range(per):
            if mine:
                @pl.when(core * per + q != d)
                def _():
                    send_part(mine, q).wait_send()
            else:
                send_part(mine, q).wait_send()


def body(core_ids, bag_lengths, first_core, middle_core, last_core, grad_hidden):
    nd, nt = lax.axis_size("dp"), lax.axis_size("table")
    block, hidden = grad_hidden.shape
    ncore = middle_core.shape[1]
    ids = jnp.transpose(core_ids, (1, 2, 3, 0))
    lengths = jnp.transpose(bag_lengths)
    cols = hidden // nd
    half = hidden // 2
    vmem = pl.BlockSpec(memory_space=pltpu.VMEM)
    hbm = pl.BlockSpec(memory_space=pltpu.HBM)
    dma = pltpu.SemaphoreType.DMA
    padded = ncore // 16 * 16 + 16
    return pl.pallas_call(
        functools.partial(kernel, nd, nt),
        out_shape=(
            jax.ShapeDtypeStruct((block, nt * WIDTH), BF16),
            jax.ShapeDtypeStruct((WIDTH, cols), F32),
        ),
        in_specs=[hbm] * 6,
        out_specs=(vmem, vmem),
        scratch_shapes=[
            pltpu.VMEM(ids.shape, jnp.int32),
            pltpu.VMEM(lengths.shape, jnp.int32),
            pltpu.VMEM((nt, 8, block), jnp.int32),
            pltpu.VMEM((nt, 8, block), jnp.int32),
            pltpu.SMEM((2, 8, block), jnp.int32),
            pltpu.VMEM((ncore, RANK, D2 * RANK), BF16),
            pltpu.VMEM((2, ncore, D1 * RANK), BF16),
            pltpu.VMEM((nt, block, half), BF16),
            pltpu.VMEM((nt, block, WIDTH), BF16),
            pltpu.VMEM((nt, block, WIDTH), BF16),
            pltpu.VMEM((padded, D1, LANES), F32),
            pltpu.VMEM((padded * D2 * D3, LANES), F32),
            pltpu.VMEM((padded, D2 * D3, LANES), BF16),
            pltpu.VMEM((block, LANES), F32),
            pltpu.VMEM((block, WIDTH), F32),
            pltpu.VMEM((2, nd // 2, WIDTH, cols), BF16),
            pltpu.VMEM((nd, WIDTH, cols), BF16),
            dma((2,)), dma, dma((2,)), dma, dma((2,)),
            dma((nt,)), dma((nt,)), dma((nt,)), dma((nt,)), dma((nt,)), dma((nt,)),
            dma((nt,)), dma((nt,)), dma((2, nd // 2)), dma((nd,)),
        ],
        compiler_params=pltpu.CompilerParams(
            collective_id=0, has_side_effects=True, vmem_limit_bytes=60 * 1024 * 1024
        ),
        cost_estimate=pl.CostEstimate(flops=2 * 10**9, bytes_accessed=6 * 10**6, transcendentals=0),
    )(ids, lengths, first_core[0], middle_core[0], last_core[0], grad_hidden)


def solution(mesh):
    placed = (
        P(("dp", "table"), None, None, None),
        P(("dp", "table"), None),
        P("table", None, None),
        P("table", None, None, None),
        P("table", None, None),
        P(("dp", "table"), None),
    )
    return jax.shard_map(
        body,
        mesh=mesh,
        in_specs=placed,
        out_specs=(P(("dp", "table"), None), P("table", "dp")),
        check_vma=False,
    )
```

```python
import functools

import jax
import jax.numpy as jnp
from jax import lax
from jax.experimental import pallas as pl
from jax.experimental.pallas import tpu as pltpu
from jax.sharding import PartitionSpec as P

D1 = 8
D2 = 2
D3 = 8
RANK = 64
BAG = 2
LANES = 128
WIDTH = D1 * D2 * D3
SPAN = D1 * LANES
LAG = 2
MESH = pl.DeviceIdType.MESH
F32 = jnp.float32
BF16 = jnp.bfloat16


def iota(shape, dim):
    return lax.broadcasted_iota(jnp.int32, shape, dim)


def spread_tables(first, last, firstx, wide, lastx):
    ncore, length = first.shape
    wide[0 : firstx.shape[0] * D1] = jnp.zeros((firstx.shape[0] * D1, LANES), F32)
    lower = iota((ncore, LANES), 1) < RANK
    for a in range(0, D1, 2):
        both = first[:, a * RANK : (a + 2) * RANK].astype(F32)
        turned = pltpu.roll(both, RANK, 1)
        wide[pl.ds(a, ncore, stride=D1), :] = jnp.where(lower, both, turned)
        wide[pl.ds(a + 1, ncore, stride=D1), :] = jnp.where(lower, turned, both)
    firstx[...] = wide[0 : firstx.shape[0] * D1].reshape(firstx.shape)
    row, lane = iota((length, 2 * LANES), 0), iota((length, 2 * LANES), 1)
    want = row - lax.rem(lane, RANK) * D3 - lane // LANES
    for c in range(0, D3, 2):
        pick = (want == c).astype(F32).astype(BF16)
        found = jnp.dot(last[...], pick, preferred_element_type=F32)
        for e in range(2):
            one = found[:, e * LANES : (e + 1) * LANES]
            wide[pl.ds(c + e, ncore, stride=D2 * D3), :] = jnp.where(lower, one, 0.0)
            wide[pl.ds(D3 + c + e, ncore, stride=D2 * D3), :] = jnp.where(lower, 0.0, one)
    lastx[...] = wide[...].reshape(lastx.shape).astype(BF16)


def heads_of(smem, slot, firstx, middle, at):
    upper = (iota((8, LANES), 1) >= RANK).astype(F32)
    lower = 1.0 - upper
    zero = jnp.zeros((16, LANES), BF16)
    groups = []
    for g in range(2):
        lefts, rights = [], []
        for j in range(BAG):
            heads, centres = [], []
            for i in range(4):
                n = at + g * 4 + i
                heads.append(firstx[smem[slot, j, n]] * (upper if i % 2 else lower))
                centres.append(middle[smem[slot, 2 + j, n]])
            top = jnp.concatenate(heads[:2], axis=0).astype(BF16)
            low = jnp.concatenate(heads[2:], axis=0).astype(BF16)
            lefts.append(jnp.concatenate([top, zero], axis=1))
            lefts.append(jnp.concatenate([zero, low], axis=1))
            rights.append(jnp.concatenate(centres, axis=0))
        both = jnp.dot(jnp.concatenate(lefts, axis=0), jnp.concatenate(rights, axis=1),
                       preferred_element_type=F32)
        groups.append(jnp.concatenate(
            [both[j * 32 : (j + 1) * 32, j * LANES : (j + 1) * LANES] for j in range(BAG)], axis=1
        ).astype(BF16))
    return jnp.concatenate(groups, axis=0)


def tails_of(smem, slot, prefix, lastx, at):
    sides = []
    for j in range(BAG):
        tails = []
        for i in range(8):
            tails.append(lastx[smem[slot, 4 + j, at + i]])
        sides.append(jnp.concatenate(tails, axis=0))
    out = lax.dot_general(prefix, jnp.concatenate(sides, axis=1), (((1,), (1,)), ((), ())),
                          preferred_element_type=F32)
    owner = iota((8, LANES), 1) // 16
    total = out[0:8]
    for i in range(1, 8):
        total = jnp.where(owner == i, out[i * 8 : (i + 1) * 8], total)
    return total


def lookups(smem, slot, firstx, middle, lastx, found, ordered, block):
    prefixes = {}
    count = block // 8
    before = found[...].astype(BF16)
    for g in range(count + LAG):
        if g == 2 * LAG:
            done = unfold(before, ordered, block)
        if g < count:
            prefixes[g] = heads_of(smem, slot, firstx, middle, g * 8)
        if g >= LAG:
            h = g - LAG
            found[h * 8 : (h + 1) * 8, :] = tails_of(smem, slot, prefixes.pop(h), lastx, h * 8)
    return done


def unfold(values, ordered, block):
    count = block // 8
    row, col = iota((LANES, SPAN), 0), iota((LANES, SPAN), 1)
    copies = jnp.logical_and(row // 16 == col // LANES, lax.rem(row, 16) == lax.rem(col, 16))
    copied = jnp.dot(values, copies.astype(F32).astype(BF16), preferred_element_type=F32)
    row, col = iota((block, LANES), 0), iota((block, LANES), 1)
    keep = (lax.rem(row, 8) == col // 16).astype(F32)
    kept = jnp.concatenate(
        [copied[:, i * LANES : (i + 1) * LANES] * keep for i in range(8)], axis=1).astype(BF16)
    add = (iota((count, block), 1) // 8 == iota((count, block), 0)).astype(F32).astype(BF16)
    sums = jnp.dot(add, kept, preferred_element_type=F32)
    for i in range(8):
        ordered[pl.ds(i, count, stride=8), :] = sums[:, i * LANES : (i + 1) * LANES]
    return ordered[...].astype(BF16)


def kernel(nd, nt, core_ids, lengths, first, middle, last, grad, pooled, wg,
           raw_ids, raw_lengths, tiles, ids, smem, mid, ends, grads, rows, sib, firstx, wide, lastx, found, ordered, part, partin,
           raw_sem, mid_sem, end_sem, own_sem, smem_sem, ids_ss, ids_rs, grad_ss, grad_rs, pool_ss, pool_rs, sib_ss, sib_rs,
           part_ss, part_rs):
    d, t = lax.axis_index("dp"), lax.axis_index("table")
    core = lax.rem(t, 2)
    pair = t - core
    other = pair + 1 - core
    block = grad.shape[0]
    ncore = middle.shape[0]
    half = grads.shape[2]
    cols = wg.shape[1]
    per = nd // 2

    load = pltpu.make_async_copy(middle, mid, mid_sem)
    loads = [pltpu.make_async_copy(ref, ends.at[k], end_sem.at[k]) for k, ref in enumerate((first, last))]
    raws = [pltpu.make_async_copy(core_ids, raw_ids, raw_sem.at[0]),
            pltpu.make_async_copy(lengths, raw_lengths, raw_sem.at[1])]
    for copy in raws + loads:
        copy.start()
    load.start()

    barrier = pltpu.get_barrier_semaphore()
    for k in range(1, nt):
        pl.semaphore_signal(barrier, inc=1, device_id=(d, lax.rem(t + k, nt)), device_id_type=MESH)
    for k in range(1, nd):
        for e in range(2):
            pl.semaphore_signal(
                barrier, inc=1, device_id=(lax.rem(d + k, nd), pair + e), device_id_type=MESH
            )
    own = pltpu.make_async_copy(
        grad.at[:, pl.ds(pl.multiple_of(core * half, LANES), half)], grads.at[t], own_sem)
    own.start()
    for copy in raws:
        copy.wait()
    slots = iota((BAG, block), 0)
    for k in range(nt):
        live = slots < raw_lengths[k : k + 1, :]
        tiles[k, 0:BAG] = jnp.where(live, raw_ids[k, 0], ncore)
        tiles[k, BAG : 2 * BAG] = raw_ids[k, 1]
        tiles[k, 2 * BAG : 3 * BAG] = raw_ids[k, 2]
        tiles[k, 3 * BAG :] = jnp.zeros((8 - 3 * BAG, block), jnp.int32)
    pltpu.make_async_copy(tiles.at[t], smem.at[0], smem_sem.at[0]).start()
    for copy in loads:
        copy.wait()
    spread_tables(ends.at[0], ends.at[1], firstx, wide, lastx)
    pl.semaphore_wait(barrier, nt - 1 + 2 * (nd - 1))

    def send_ids(k):
        peer = lax.rem(t + k, nt)
        return pltpu.make_async_remote_copy(
            tiles.at[peer], ids.at[t], ids_ss.at[k], ids_rs.at[k],
            device_id=(d, peer), device_id_type=MESH)

    def send_grad(k):
        peer = lax.rem(t + k, nt)
        mine = pl.ds(pl.multiple_of(lax.rem(peer, 2) * half, LANES), half)
        return pltpu.make_async_remote_copy(
            grad.at[:, mine], grads.at[t], grad_ss.at[k], grad_rs.at[k],
            device_id=(d, peer), device_id_type=MESH)

    def send_pooled(k):
        peer = lax.rem(t - k + nt, nt)
        return pltpu.make_async_remote_copy(
            rows.at[peer], pooled.at[:, pl.ds(pl.multiple_of(t * WIDTH, LANES), WIDTH)],
            pool_ss.at[k], pool_rs.at[k], device_id=(d, peer), device_id_type=MESH)

    def send_sib(k):
        peer = lax.rem(t - k + nt, nt)
        return pltpu.make_async_remote_copy(
            rows.at[peer], sib.at[peer], sib_ss.at[peer], sib_rs.at[peer],
            device_id=(d, other), device_id_type=MESH)

    for k in range(1, nt):
        send_ids(k).start()
    for k in range(1, nt):
        send_grad(k).start()
    load.wait()

    def chunk(k, carry):
        s = lax.rem(t - k + nt, nt)
        slot = lax.rem(k, 2)
        pltpu.make_async_copy(ids.at[s], smem.at[slot], smem_sem.at[slot]).wait()

        @pl.when(k + 1 < nt)
        def _():
            after = lax.rem(t - k - 1 + nt, nt)
            pltpu.make_async_remote_copy(
                ids.at[after], ids.at[after], ids_ss.at[k + 1], ids_rs.at[k + 1],
                device_id=(d, other), device_id_type=MESH).wait_recv()
            pltpu.make_async_copy(ids.at[after], smem.at[1 - slot], smem_sem.at[1 - slot]).start()

        rows[lax.rem(s + 1, nt)] = lookups(smem, slot, firstx, mid, lastx, found, ordered, block)

        @pl.when(k > 0)
        def _():
            send_sib(k - 1).start()

        @pl.when(k > 1)
        def _():
            send_pooled(k - 1).start()

        return carry

    lax.fori_loop(0, nt, chunk, 0)
    rows[lax.rem(t + 1, nt)] = unfold(found[...].astype(BF16), ordered, block)
    send_sib(nt - 1).start()
    send_pooled(nt - 1).start()
    pooled[:, pl.ds(pl.multiple_of(t * WIDTH, LANES), WIDTH)] = rows[t]
    own.wait()

    for k in range(1, nt):
        s = lax.rem(t - k + nt, nt)
        pltpu.make_async_remote_copy(
            grads.at[s], grads.at[s], grad_ss.at[k], grad_rs.at[k],
            device_id=(d, other), device_id_type=MESH).wait_recv()
    for s in range(nt):
        pltpu.make_async_remote_copy(
            sib.at[s], sib.at[s], sib_ss.at[s], sib_rs.at[s],
            device_id=(d, other), device_id_type=MESH).wait_recv()

    group = nt * block

    def partial(mine):
        left = rows if mine else sib
        return lax.dot_general(
            left[...].reshape(group, WIDTH), grads[...].reshape(group, half),
            (((0,), (0,)), ((), ())), preferred_element_type=F32).astype(BF16)

    def send_part(mine, q):
        target = core * per + q
        return pltpu.make_async_remote_copy(
            part.at[mine, q], partin.at[d], part_ss.at[mine, q], part_rs.at[d],
            device_id=(target, t if mine else other), device_id_type=MESH)

    for mine in (1, 0):
        whole = partial(mine)
        for q in range(per):
            part[mine, q] = whole[:, q * cols : (q + 1) * cols]
            if mine:
                @pl.when(core * per + q != d)
                def _():
                    send_part(mine, q).start()

                @pl.when(core * per + q == d)
                def _():
                    partin[d] = part[mine, q]
            else:
                send_part(mine, q).start()

    for k in range(1, nt):
        send_ids(k).wait_send()
        send_grad(k).wait_send()
        send_pooled(k).wait_send()
        s = lax.rem(t + k, nt)
        pltpu.make_async_remote_copy(
            rows.at[s], pooled.at[:, pl.ds(pl.multiple_of(s * WIDTH, LANES), WIDTH)],
            pool_ss.at[k], pool_rs.at[k], device_id=(d, other), device_id_type=MESH).wait_recv()
    for k in range(nt):
        send_sib(k).wait_send()

    source = d // per
    for k in range(nd):
        @pl.when(jnp.logical_or(source != core, k != d))
        def _():
            pltpu.make_async_remote_copy(
                partin.at[k], partin.at[k], part_ss.at[0, 0], part_rs.at[k],
                device_id=(d, other), device_id_type=MESH).wait_recv()
    total = partin[0].astype(F32)
    for k in range(1, nd):
        total = total + partin[k].astype(F32)
    wg[...] = total
    for mine in (1, 0):
        for q in range(per):
            if mine:
                @pl.when(core * per + q != d)
                def _():
                    send_part(mine, q).wait_send()
            else:
                send_part(mine, q).wait_send()


def body(core_ids, bag_lengths, first_core, middle_core, last_core, grad_hidden):
    nd, nt = lax.axis_size("dp"), lax.axis_size("table")
    block, hidden = grad_hidden.shape
    ncore = middle_core.shape[1]
    ids = jnp.transpose(core_ids, (1, 2, 3, 0))
    lengths = jnp.transpose(bag_lengths)
    cols = hidden // nd
    half = hidden // 2
    vmem = pl.BlockSpec(memory_space=pltpu.VMEM)
    hbm = pl.BlockSpec(memory_space=pltpu.HBM)
    dma = pltpu.SemaphoreType.DMA
    padded = ncore // 16 * 16 + 16
    return pl.pallas_call(
        functools.partial(kernel, nd, nt),
        out_shape=(
            jax.ShapeDtypeStruct((block, nt * WIDTH), BF16),
            jax.ShapeDtypeStruct((WIDTH, cols), F32),
        ),
        in_specs=[hbm] * 6,
        out_specs=(vmem, vmem),
        scratch_shapes=[
            pltpu.VMEM(ids.shape, jnp.int32),
            pltpu.VMEM(lengths.shape, jnp.int32),
            pltpu.VMEM((nt, 8, block), jnp.int32),
            pltpu.VMEM((nt, 8, block), jnp.int32),
            pltpu.SMEM((2, 8, block), jnp.int32),
            pltpu.VMEM((ncore, RANK, D2 * RANK), BF16),
            pltpu.VMEM((2, ncore, D1 * RANK), BF16),
            pltpu.VMEM((nt, block, half), BF16),
            pltpu.VMEM((nt, block, WIDTH), BF16),
            pltpu.VMEM((nt, block, WIDTH), BF16),
            pltpu.VMEM((padded, D1, LANES), F32),
            pltpu.VMEM((padded * D2 * D3, LANES), F32),
            pltpu.VMEM((padded, D2 * D3, LANES), BF16),
            pltpu.VMEM((block, LANES), F32),
            pltpu.VMEM((block, WIDTH), F32),
            pltpu.VMEM((2, nd // 2, WIDTH, cols), BF16),
            pltpu.VMEM((nd, WIDTH, cols), BF16),
            dma((2,)), dma, dma((2,)), dma, dma((2,)),
            dma((nt,)), dma((nt,)), dma((nt,)), dma((nt,)), dma((nt,)), dma((nt,)),
            dma((nt,)), dma((nt,)), dma((2, nd // 2)), dma((nd,)),
        ],
        compiler_params=pltpu.CompilerParams(
            collective_id=0, has_side_effects=True, vmem_limit_bytes=54784 * 1024
        ),
        cost_estimate=pl.CostEstimate(flops=2 * 10**9, bytes_accessed=6 * 10**6, transcendentals=0),
    )(ids, lengths, first_core[0], middle_core[0], last_core[0], grad_hidden)


def solution(mesh):
    placed = (
        P(("dp", "table"), None, None, None),
        P(("dp", "table"), None),
        P("table", None, None),
        P("table", None, None, None),
        P("table", None, None),
        P(("dp", "table"), None),
    )
    return jax.shard_map(
        body,
        mesh=mesh,
        in_specs=placed,
        out_specs=(P(("dp", "table"), None), P("table", "dp")),
        check_vma=False,
    )
```

```python
import functools

import jax
import jax.numpy as jnp
from jax import lax
from jax.experimental import pallas as pl
from jax.experimental.pallas import tpu as pltpu
from jax.sharding import PartitionSpec as P

D1 = 8
D2 = 2
D3 = 8
RANK = 64
BAG = 2
LANES = 128
WIDTH = D1 * D2 * D3
SPAN = D1 * LANES
LAG = 2
MESH = pl.DeviceIdType.MESH
F32 = jnp.float32
BF16 = jnp.bfloat16


def iota(shape, dim):
    return lax.broadcasted_iota(jnp.int32, shape, dim)


def spread_tables(first, last, firstx, wide, lastx):
    ncore, length = first.shape
    wide[0 : firstx.shape[0] * D1] = jnp.zeros((firstx.shape[0] * D1, LANES), F32)
    lower = iota((ncore, LANES), 1) < RANK
    for a in range(0, D1, 2):
        both = first[:, a * RANK : (a + 2) * RANK].astype(F32)
        turned = pltpu.roll(both, RANK, 1)
        wide[pl.ds(a, ncore, stride=D1), :] = jnp.where(lower, both, turned)
        wide[pl.ds(a + 1, ncore, stride=D1), :] = jnp.where(lower, turned, both)
    firstx[...] = wide[0 : firstx.shape[0] * D1].reshape(firstx.shape)
    row, lane = iota((length, 2 * LANES), 0), iota((length, 2 * LANES), 1)
    want = row - lax.rem(lane, RANK) * D3 - lane // LANES
    for c in range(0, D3, 2):
        pick = (want == c).astype(F32).astype(BF16)
        found = jnp.dot(last[...], pick, preferred_element_type=F32)
        for e in range(2):
            one = found[:, e * LANES : (e + 1) * LANES]
            wide[pl.ds(c + e, ncore, stride=D2 * D3), :] = jnp.where(lower, one, 0.0)
            wide[pl.ds(D3 + c + e, ncore, stride=D2 * D3), :] = jnp.where(lower, 0.0, one)
    lastx[...] = wide[...].reshape(lastx.shape).astype(BF16)


def heads_of(smem, slot, firstx, middle, at):
    upper = (iota((8, LANES), 1) >= RANK).astype(F32)
    lower = 1.0 - upper
    zero = jnp.zeros((16, LANES), BF16)
    groups = []
    for g in range(2):
        lefts, rights = [], []
        for j in range(BAG):
            heads, centres = [], []
            for i in range(4):
                n = at + g * 4 + i
                heads.append(firstx[smem[slot, j, n]] * (upper if i % 2 else lower))
                centres.append(middle[smem[slot, 2 + j, n]])
            top = jnp.concatenate(heads[:2], axis=0).astype(BF16)
            low = jnp.concatenate(heads[2:], axis=0).astype(BF16)
            lefts.append(jnp.concatenate([top, zero], axis=1))
            lefts.append(jnp.concatenate([zero, low], axis=1))
            rights.append(jnp.concatenate(centres, axis=0))
        both = jnp.dot(jnp.concatenate(lefts, axis=0), jnp.concatenate(rights, axis=1),
                       preferred_element_type=F32)
        groups.append(jnp.concatenate(
            [both[j * 32 : (j + 1) * 32, j * LANES : (j + 1) * LANES] for j in range(BAG)], axis=1
        ).astype(BF16))
    return jnp.concatenate(groups, axis=0)


def tails_of(smem, slot, prefix, lastx, at):
    sides = []
    for j in range(BAG):
        tails = []
        for i in range(8):
            tails.append(lastx[smem[slot, 4 + j, at + i]])
        sides.append(jnp.concatenate(tails, axis=0))
    out = lax.dot_general(prefix, jnp.concatenate(sides, axis=1), (((1,), (1,)), ((), ())),
                          preferred_element_type=F32)
    owner = iota((8, LANES), 1) // 16
    total = out[0:8]
    for i in range(1, 8):
        total = jnp.where(owner == i, out[i * 8 : (i + 1) * 8], total)
    return total


def lookups(smem, slot, firstx, middle, lastx, found, ordered, block):
    prefixes = {}
    count = block // 8
    before = found[...].astype(BF16)
    for g in range(count + LAG):
        if g == 2 * LAG:
            done = unfold(before, ordered, block)
        if g < count:
            prefixes[g] = heads_of(smem, slot, firstx, middle, g * 8)
        if g >= LAG:
            h = g - LAG
            found[h * 8 : (h + 1) * 8, :] = tails_of(smem, slot, prefixes.pop(h), lastx, h * 8)
    return done


def unfold(values, ordered, block):
    count = block // 8
    row, col = iota((LANES, SPAN), 0), iota((LANES, SPAN), 1)
    copies = jnp.logical_and(row // 16 == col // LANES, lax.rem(row, 16) == lax.rem(col, 16))
    copied = jnp.dot(values, copies.astype(F32).astype(BF16), preferred_element_type=F32)
    row, col = iota((block, LANES), 0), iota((block, LANES), 1)
    keep = (lax.rem(row, 8) == col // 16).astype(F32)
    kept = jnp.concatenate(
        [copied[:, i * LANES : (i + 1) * LANES] * keep for i in range(8)], axis=1).astype(BF16)
    add = (iota((count, block), 1) // 8 == iota((count, block), 0)).astype(F32).astype(BF16)
    sums = jnp.dot(add, kept, preferred_element_type=F32)
    for i in range(8):
        ordered[pl.ds(i, count, stride=8), :] = sums[:, i * LANES : (i + 1) * LANES]
    return ordered[...].astype(BF16)


def kernel(nd, nt, raw_ids, first, middle, last, grad, pooled, wg,
           tiles, ids, smem, mid, ends, grads, rows, sib, firstx, wide, lastx, found, ordered, part, partin,
           mid_sem, end_sem, own_sem, smem_sem, ids_ss, ids_rs, grad_ss, grad_rs, pool_ss, pool_rs, sib_ss, sib_rs,
           part_ss, part_rs):
    d, t = lax.axis_index("dp"), lax.axis_index("table")
    core = lax.rem(t, 2)
    pair = t - core
    other = pair + 1 - core
    block = grad.shape[0]
    ncore = middle.shape[0]
    half = grads.shape[2]
    cols = wg.shape[1]
    per = nd // 2

    load = pltpu.make_async_copy(middle, mid, mid_sem)
    loads = [pltpu.make_async_copy(ref, ends.at[k], end_sem.at[k]) for k, ref in enumerate((first, last))]
    for copy in loads:
        copy.start()
    load.start()

    barrier = pltpu.get_barrier_semaphore()
    for k in range(1, nt):
        pl.semaphore_signal(barrier, inc=1, device_id=(d, lax.rem(t + k, nt)), device_id_type=MESH)
    for k in range(1, nd):
        for e in range(2):
            pl.semaphore_signal(
                barrier, inc=1, device_id=(lax.rem(d + k, nd), pair + e), device_id_type=MESH
            )
    own = pltpu.make_async_copy(
        grad.at[:, pl.ds(pl.multiple_of(core * half, LANES), half)], grads.at[t], own_sem)
    own.start()
    slots = iota((BAG, block), 0)
    for k in range(nt):
        live = slots < raw_ids[k, 3]
        tiles[k, 0:BAG] = jnp.where(live, raw_ids[k, 0], ncore)
        tiles[k, BAG : 2 * BAG] = raw_ids[k, 1]
        tiles[k, 2 * BAG : 3 * BAG] = raw_ids[k, 2]
        tiles[k, 3 * BAG :] = jnp.zeros((8 - 3 * BAG, block), jnp.int32)
    pltpu.make_async_copy(tiles.at[t], smem.at[0], smem_sem.at[0]).start()
    pl.semaphore_wait(barrier, nt - 1 + 2 * (nd - 1))

    def send_ids(k):
        peer = lax.rem(t + k, nt)
        return pltpu.make_async_remote_copy(
            tiles.at[peer], ids.at[t], ids_ss.at[k], ids_rs.at[k],
            device_id=(d, peer), device_id_type=MESH)

    def send_grad(k):
        peer = lax.rem(t + k, nt)
        mine = pl.ds(pl.multiple_of(lax.rem(peer, 2) * half, LANES), half)
        return pltpu.make_async_remote_copy(
            grad.at[:, mine], grads.at[t], grad_ss.at[k], grad_rs.at[k],
            device_id=(d, peer), device_id_type=MESH)

    def send_pooled(k):
        peer = lax.rem(t - k + nt, nt)
        return pltpu.make_async_remote_copy(
            rows.at[peer], pooled.at[:, pl.ds(pl.multiple_of(t * WIDTH, LANES), WIDTH)],
            pool_ss.at[k], pool_rs.at[k], device_id=(d, peer), device_id_type=MESH)

    def send_sib(k):
        peer = lax.rem(t - k + nt, nt)
        return pltpu.make_async_remote_copy(
            rows.at[peer], sib.at[peer], sib_ss.at[peer], sib_rs.at[peer],
            device_id=(d, other), device_id_type=MESH)

    for k in range(1, nt):
        send_ids(k).start()
    for k in range(1, nt):
        send_grad(k).start()
    for copy in loads:
        copy.wait()
    spread_tables(ends.at[0], ends.at[1], firstx, wide, lastx)
    load.wait()

    def chunk(k, carry):
        s = lax.rem(t - k + nt, nt)
        slot = lax.rem(k, 2)
        pltpu.make_async_copy(ids.at[s], smem.at[slot], smem_sem.at[slot]).wait()

        @pl.when(k + 1 < nt)
        def _():
            after = lax.rem(t - k - 1 + nt, nt)
            pltpu.make_async_remote_copy(
                ids.at[after], ids.at[after], ids_ss.at[k + 1], ids_rs.at[k + 1],
                device_id=(d, other), device_id_type=MESH).wait_recv()
            pltpu.make_async_copy(ids.at[after], smem.at[1 - slot], smem_sem.at[1 - slot]).start()

        rows[lax.rem(s + 1, nt)] = lookups(smem, slot, firstx, mid, lastx, found, ordered, block)

        @pl.when(k > 0)
        def _():
            send_sib(k - 1).start()

        @pl.when(k > 1)
        def _():
            send_pooled(k - 1).start()

        return carry

    lax.fori_loop(0, nt, chunk, 0)
    rows[lax.rem(t + 1, nt)] = unfold(found[...].astype(BF16), ordered, block)
    send_sib(nt - 1).start()
    send_pooled(nt - 1).start()
    pooled[:, pl.ds(pl.multiple_of(t * WIDTH, LANES), WIDTH)] = rows[t]
    own.wait()

    for k in range(1, nt):
        s = lax.rem(t - k + nt, nt)
        pltpu.make_async_remote_copy(
            grads.at[s], grads.at[s], grad_ss.at[k], grad_rs.at[k],
            device_id=(d, other), device_id_type=MESH).wait_recv()
    group = nt * block

    def partial(mine):
        left = rows if mine else sib
        return lax.dot_general(
            left[...].reshape(group, WIDTH), grads[...].reshape(group, half),
            (((0,), (0,)), ((), ())), preferred_element_type=F32).astype(BF16)

    def send_part(mine, q):
        target = core * per + q
        return pltpu.make_async_remote_copy(
            part.at[mine, q], partin.at[d], part_ss.at[mine, q], part_rs.at[d],
            device_id=(target, t if mine else other), device_id_type=MESH)

    for mine in (1, 0):
        if not mine:
            for s in range(nt):
                pltpu.make_async_remote_copy(
                    sib.at[s], sib.at[s], sib_ss.at[s], sib_rs.at[s],
                    device_id=(d, other), device_id_type=MESH).wait_recv()
        whole = partial(mine)
        for q in range(per):
            part[mine, q] = whole[:, q * cols : (q + 1) * cols]
            if mine:
                @pl.when(core * per + q != d)
                def _():
                    send_part(mine, q).start()

                @pl.when(core * per + q == d)
                def _():
                    partin[d] = part[mine, q]
            else:
                send_part(mine, q).start()

    for k in range(1, nt):
        send_ids(k).wait_send()
        send_grad(k).wait_send()
        send_pooled(k).wait_send()
        s = lax.rem(t + k, nt)
        pltpu.make_async_remote_copy(
            rows.at[s], pooled.at[:, pl.ds(pl.multiple_of(s * WIDTH, LANES), WIDTH)],
            pool_ss.at[k], pool_rs.at[k], device_id=(d, other), device_id_type=MESH).wait_recv()
    for k in range(nt):
        send_sib(k).wait_send()

    source = d // per
    for k in range(nd):
        @pl.when(jnp.logical_or(source != core, k != d))
        def _():
            pltpu.make_async_remote_copy(
                partin.at[k], partin.at[k], part_ss.at[0, 0], part_rs.at[k],
                device_id=(d, other), device_id_type=MESH).wait_recv()
    total = partin[0].astype(F32)
    for k in range(1, nd):
        total = total + partin[k].astype(F32)
    wg[...] = total
    for mine in (1, 0):
        for q in range(per):
            if mine:
                @pl.when(core * per + q != d)
                def _():
                    send_part(mine, q).wait_send()
            else:
                send_part(mine, q).wait_send()


def body(core_ids, bag_lengths, first_core, middle_core, last_core, grad_hidden):
    nd, nt = lax.axis_size("dp"), lax.axis_size("table")
    block, hidden = grad_hidden.shape
    ncore = middle_core.shape[1]
    lengths = jnp.broadcast_to(jnp.transpose(bag_lengths)[:, None, None, :], (nt, 1, BAG, block))
    ids = jnp.concatenate([jnp.transpose(core_ids, (1, 2, 3, 0)), lengths], axis=1)
    cols = hidden // nd
    half = hidden // 2
    vmem = pl.BlockSpec(memory_space=pltpu.VMEM)
    hbm = pl.BlockSpec(memory_space=pltpu.HBM)
    dma = pltpu.SemaphoreType.DMA
    padded = ncore // 16 * 16 + 16
    return pl.pallas_call(
        functools.partial(kernel, nd, nt),
        out_shape=(
            jax.ShapeDtypeStruct((block, nt * WIDTH), BF16),
            jax.ShapeDtypeStruct((WIDTH, cols), F32),
        ),
        in_specs=[vmem] + [hbm] * 4,
        out_specs=(vmem, vmem),
        scratch_shapes=[
            pltpu.VMEM((nt, 8, block), jnp.int32),
            pltpu.VMEM((nt, 8, block), jnp.int32),
            pltpu.SMEM((2, 8, block), jnp.int32),
            pltpu.VMEM((ncore, RANK, D2 * RANK), BF16),
            pltpu.VMEM((2, ncore, D1 * RANK), BF16),
            pltpu.VMEM((nt, block, half), BF16),
            pltpu.VMEM((nt, block, WIDTH), BF16),
            pltpu.VMEM((nt, block, WIDTH), BF16),
            pltpu.VMEM((padded, D1, LANES), F32),
            pltpu.VMEM((padded * D2 * D3, LANES), F32),
            pltpu.VMEM((padded, D2 * D3, LANES), BF16),
            pltpu.VMEM((block, LANES), F32),
            pltpu.VMEM((block, WIDTH), F32),
            pltpu.VMEM((2, nd // 2, WIDTH, cols), BF16),
            pltpu.VMEM((nd, WIDTH, cols), BF16),
            dma, dma((2,)), dma, dma((2,)),
            dma((nt,)), dma((nt,)), dma((nt,)), dma((nt,)), dma((nt,)), dma((nt,)),
            dma((nt,)), dma((nt,)), dma((2, nd // 2)), dma((nd,)),
        ],
        compiler_params=pltpu.CompilerParams(
            collective_id=0, has_side_effects=True, vmem_limit_bytes=54784 * 1024
        ),
        cost_estimate=pl.CostEstimate(flops=2 * 10**9, bytes_accessed=6 * 10**6, transcendentals=0),
    )(ids, first_core[0], middle_core[0], last_core[0], grad_hidden)


def solution(mesh):
    placed = (
        P(("dp", "table"), None, None, None),
        P(("dp", "table"), None),
        P("table", None, None),
        P("table", None, None, None),
        P("table", None, None),
        P(("dp", "table"), None),
    )
    return jax.shard_map(
        body,
        mesh=mesh,
        in_specs=placed,
        out_specs=(P(("dp", "table"), None), P("table", "dp")),
        check_vma=False,
    )
```

```python
import functools

import jax
import jax.numpy as jnp
from jax import lax
from jax.experimental import pallas as pl
from jax.experimental.pallas import tpu as pltpu
from jax.sharding import PartitionSpec as P

D1 = 8
D2 = 2
D3 = 8
RANK = 64
BAG = 2
LANES = 128
WIDTH = D1 * D2 * D3
SPAN = D1 * LANES
LAG = 2
MESH = pl.DeviceIdType.MESH
F32 = jnp.float32
BF16 = jnp.bfloat16


def iota(shape, dim):
    return lax.broadcasted_iota(jnp.int32, shape, dim)


def spread_tables(first, last, firstx, wide, lastx):
    ncore, length = first.shape
    wide[0 : firstx.shape[0] * D1] = jnp.zeros((firstx.shape[0] * D1, LANES), F32)
    lower = iota((ncore, LANES), 1) < RANK
    for a in range(0, D1, 2):
        both = first[:, a * RANK : (a + 2) * RANK].astype(F32)
        turned = pltpu.roll(both, RANK, 1)
        wide[pl.ds(a, ncore, stride=D1), :] = jnp.where(lower, both, turned)
        wide[pl.ds(a + 1, ncore, stride=D1), :] = jnp.where(lower, turned, both)
    firstx[...] = wide[0 : firstx.shape[0] * D1].reshape(firstx.shape)
    row, lane = iota((length, 2 * LANES), 0), iota((length, 2 * LANES), 1)
    want = row - lax.rem(lane, RANK) * D3 - lane // LANES
    for c in range(0, D3, 2):
        pick = (want == c).astype(F32).astype(BF16)
        found = jnp.dot(last[...], pick, preferred_element_type=F32)
        for e in range(2):
            one = found[:, e * LANES : (e + 1) * LANES]
            wide[pl.ds(c + e, ncore, stride=D2 * D3), :] = jnp.where(lower, one, 0.0)
            wide[pl.ds(D3 + c + e, ncore, stride=D2 * D3), :] = jnp.where(lower, 0.0, one)
    lastx[...] = wide[...].reshape(lastx.shape).astype(BF16)


def heads_of(smem, slot, firstx, middle, at):
    upper = (iota((8, LANES), 1) >= RANK).astype(F32)
    lower = 1.0 - upper
    zero = jnp.zeros((16, LANES), BF16)
    groups = []
    for g in range(2):
        lefts, rights = [], []
        for j in range(BAG):
            heads, centres = [], []
            for i in range(4):
                n = at + g * 4 + i
                heads.append(firstx[smem[slot, j, n]] * (upper if i % 2 else lower))
                centres.append(middle[smem[slot, 2 + j, n]])
            top = jnp.concatenate(heads[:2], axis=0).astype(BF16)
            low = jnp.concatenate(heads[2:], axis=0).astype(BF16)
            lefts.append(jnp.concatenate([top, zero], axis=1))
            lefts.append(jnp.concatenate([zero, low], axis=1))
            rights.append(jnp.concatenate(centres, axis=0))
        both = jnp.dot(jnp.concatenate(lefts, axis=0), jnp.concatenate(rights, axis=1),
                       preferred_element_type=F32)
        groups.append(jnp.concatenate(
            [both[j * 32 : (j + 1) * 32, j * LANES : (j + 1) * LANES] for j in range(BAG)], axis=1
        ).astype(BF16))
    return jnp.concatenate(groups, axis=0)


def tails_of(smem, slot, prefix, lastx, at):
    sides = []
    for j in range(BAG):
        tails = []
        for i in range(8):
            tails.append(lastx[smem[slot, 4 + j, at + i]])
        sides.append(jnp.concatenate(tails, axis=0))
    out = lax.dot_general(prefix, jnp.concatenate(sides, axis=1), (((1,), (1,)), ((), ())),
                          preferred_element_type=F32)
    owner = iota((8, LANES), 1) // 16
    total = out[0:8]
    for i in range(1, 8):
        total = jnp.where(owner == i, out[i * 8 : (i + 1) * 8], total)
    return total


def finish(smem, slot, lastx, kept, found, block):
    for e in range(LAG):
        h = block // 8 - LAG + e
        found[h * 8 : (h + 1) * 8, :] = tails_of(smem, slot, kept[e], lastx, h * 8)


def lookups(smem, slot, old, firstx, middle, lastx, kept, found, ordered, block):
    count = block // 8
    prefixes = {g: heads_of(smem, slot, firstx, middle, g * 8) for g in range(LAG)}
    finish(smem, old, lastx, kept, found, block)
    before = found[...].astype(BF16)
    for g in range(LAG, count):
        prefixes[g] = heads_of(smem, slot, firstx, middle, g * 8)
        h = g - LAG
        found[h * 8 : (h + 1) * 8, :] = tails_of(smem, slot, prefixes.pop(h), lastx, h * 8)
        if g == 2 * LAG:
            done = unfold(before, ordered, block)
    for e in range(LAG):
        kept[e] = prefixes.pop(count - LAG + e)
    return done


def unfold(values, ordered, block):
    count = block // 8
    row, col = iota((LANES, SPAN), 0), iota((LANES, SPAN), 1)
    copies = jnp.logical_and(row // 16 == col // LANES, lax.rem(row, 16) == lax.rem(col, 16))
    copied = jnp.dot(values, copies.astype(F32).astype(BF16), preferred_element_type=F32)
    row, col = iota((block, LANES), 0), iota((block, LANES), 1)
    keep = (lax.rem(row, 8) == col // 16).astype(F32)
    kept = jnp.concatenate(
        [copied[:, i * LANES : (i + 1) * LANES] * keep for i in range(8)], axis=1).astype(BF16)
    add = (iota((count, block), 1) // 8 == iota((count, block), 0)).astype(F32).astype(BF16)
    sums = jnp.dot(add, kept, preferred_element_type=F32)
    for i in range(8):
        ordered[pl.ds(i, count, stride=8), :] = sums[:, i * LANES : (i + 1) * LANES]
    return ordered[...].astype(BF16)


def kernel(nd, nt, raw_ids, first, middle, last, grad, pooled, wg,
           tiles, ids, smem, mid, ends, grads, rows, sib, firstx, wide, lastx, kept, found, ordered, part, partin,
           mid_sem, end_sem, own_sem, smem_sem, ids_ss, ids_rs, grad_ss, grad_rs, pool_ss, pool_rs, sib_ss, sib_rs,
           part_ss, part_rs):
    d, t = lax.axis_index("dp"), lax.axis_index("table")
    core = lax.rem(t, 2)
    pair = t - core
    other = pair + 1 - core
    block = grad.shape[0]
    half = grads.shape[2]
    cols = wg.shape[1]
    per = nd // 2

    load = pltpu.make_async_copy(middle, mid, mid_sem)
    loads = [pltpu.make_async_copy(ref, ends.at[k], end_sem.at[k]) for k, ref in enumerate((first, last))]
    for copy in loads:
        copy.start()
    load.start()

    barrier = pltpu.get_barrier_semaphore()
    for k in range(1, nt):
        pl.semaphore_signal(barrier, inc=1, device_id=(d, lax.rem(t + k, nt)), device_id_type=MESH)
    for k in range(1, nd):
        for e in range(2):
            pl.semaphore_signal(
                barrier, inc=1, device_id=(lax.rem(d + k, nd), pair + e), device_id_type=MESH
            )
    own = pltpu.make_async_copy(
        grad.at[:, pl.ds(pl.multiple_of(core * half, LANES), half)], grads.at[t], own_sem)
    own.start()
    for k in range(nt):
        tiles[k, 0:BAG] = raw_ids[k, 0]
        tiles[k, BAG : 2 * BAG] = raw_ids[k, 1]
        tiles[k, 2 * BAG : 3 * BAG] = raw_ids[k, 2]
        tiles[k, 3 * BAG :] = jnp.zeros((8 - 3 * BAG, block), jnp.int32)
    pltpu.make_async_copy(tiles.at[t], smem.at[0], smem_sem.at[0]).start()
    blank = pltpu.make_async_copy(tiles.at[t], smem.at[2], smem_sem.at[2])
    blank.start()
    kept[...] = jnp.zeros_like(kept)
    found[...] = jnp.zeros_like(found)
    pl.semaphore_wait(barrier, nt - 1 + 2 * (nd - 1))

    def send_ids(k):
        peer = lax.rem(t + k, nt)
        return pltpu.make_async_remote_copy(
            tiles.at[peer], ids.at[t], ids_ss.at[k], ids_rs.at[k],
            device_id=(d, peer), device_id_type=MESH)

    def send_grad(k):
        peer = lax.rem(t + k, nt)
        mine = pl.ds(pl.multiple_of(lax.rem(peer, 2) * half, LANES), half)
        return pltpu.make_async_remote_copy(
            grad.at[:, mine], grads.at[t], grad_ss.at[k], grad_rs.at[k],
            device_id=(d, peer), device_id_type=MESH)

    def send_pooled(k):
        peer = lax.rem(t - k + nt, nt)
        return pltpu.make_async_remote_copy(
            rows.at[peer], pooled.at[:, pl.ds(pl.multiple_of(t * WIDTH, LANES), WIDTH)],
            pool_ss.at[k], pool_rs.at[k], device_id=(d, peer), device_id_type=MESH)

    def send_sib(k):
        peer = lax.rem(t - k + nt, nt)
        return pltpu.make_async_remote_copy(
            rows.at[peer], sib.at[peer], sib_ss.at[peer], sib_rs.at[peer],
            device_id=(d, other), device_id_type=MESH)

    for k in range(1, nt):
        send_ids(k).start()
    for k in range(1, nt):
        send_grad(k).start()
    for copy in loads:
        copy.wait()
    spread_tables(ends.at[0], ends.at[1], firstx, wide, lastx)
    load.wait()
    blank.wait()

    def chunk(k, carry):
        s = lax.rem(t - k + nt, nt)
        slot, after_slot, old = lax.rem(k, 3), lax.rem(k + 1, 3), lax.rem(k + 2, 3)
        pltpu.make_async_copy(ids.at[s], smem.at[slot], smem_sem.at[slot]).wait()

        @pl.when(k + 1 < nt)
        def _():
            after = lax.rem(t - k - 1 + nt, nt)
            pltpu.make_async_remote_copy(
                ids.at[after], ids.at[after], ids_ss.at[k + 1], ids_rs.at[k + 1],
                device_id=(d, other), device_id_type=MESH).wait_recv()
            pltpu.make_async_copy(ids.at[after], smem.at[after_slot], smem_sem.at[after_slot]).start()

        rows[lax.rem(s + 1, nt)] = lookups(
            smem, slot, old, firstx, mid, lastx, kept, found, ordered, block)

        @pl.when(k > 0)
        def _():
            send_sib(k - 1).start()

        @pl.when(k > 1)
        def _():
            send_pooled(k - 1).start()

        return carry

    lax.fori_loop(0, nt, chunk, 0)
    finish(smem, lax.rem(nt - 1, 3), lastx, kept, found, block)
    rows[lax.rem(t + 1, nt)] = unfold(found[...].astype(BF16), ordered, block)
    send_sib(nt - 1).start()
    send_pooled(nt - 1).start()
    pooled[:, pl.ds(pl.multiple_of(t * WIDTH, LANES), WIDTH)] = rows[t]
    own.wait()

    for k in range(1, nt):
        s = lax.rem(t - k + nt, nt)
        pltpu.make_async_remote_copy(
            grads.at[s], grads.at[s], grad_ss.at[k], grad_rs.at[k],
            device_id=(d, other), device_id_type=MESH).wait_recv()
    group = nt * block

    def partial(mine):
        left = rows if mine else sib
        return lax.dot_general(
            left[...].reshape(group, WIDTH), grads[...].reshape(group, half),
            (((0,), (0,)), ((), ())), preferred_element_type=F32).astype(BF16)

    def send_part(mine, q):
        target = core * per + q
        return pltpu.make_async_remote_copy(
            part.at[mine, q], partin.at[d], part_ss.at[mine, q], part_rs.at[d],
            device_id=(target, t if mine else other), device_id_type=MESH)

    for mine in (1, 0):
        if not mine:
            for s in range(nt):
                pltpu.make_async_remote_copy(
                    sib.at[s], sib.at[s], sib_ss.at[s], sib_rs.at[s],
                    device_id=(d, other), device_id_type=MESH).wait_recv()
        whole = partial(mine)
        for q in range(per):
            part[mine, q] = whole[:, q * cols : (q + 1) * cols]
            if mine:
                @pl.when(core * per + q != d)
                def _():
                    send_part(mine, q).start()

                @pl.when(core * per + q == d)
                def _():
                    partin[d] = part[mine, q]
            else:
                send_part(mine, q).start()

    for k in range(1, nt):
        send_ids(k).wait_send()
        send_grad(k).wait_send()
        send_pooled(k).wait_send()
        s = lax.rem(t + k, nt)
        pltpu.make_async_remote_copy(
            rows.at[s], pooled.at[:, pl.ds(pl.multiple_of(s * WIDTH, LANES), WIDTH)],
            pool_ss.at[k], pool_rs.at[k], device_id=(d, other), device_id_type=MESH).wait_recv()
    for k in range(nt):
        send_sib(k).wait_send()

    source = d // per
    for k in range(nd):
        @pl.when(jnp.logical_or(source != core, k != d))
        def _():
            pltpu.make_async_remote_copy(
                partin.at[k], partin.at[k], part_ss.at[0, 0], part_rs.at[k],
                device_id=(d, other), device_id_type=MESH).wait_recv()
    total = partin[0].astype(F32)
    for k in range(1, nd):
        total = total + partin[k].astype(F32)
    wg[...] = total
    for mine in (1, 0):
        for q in range(per):
            if mine:
                @pl.when(core * per + q != d)
                def _():
                    send_part(mine, q).wait_send()
            else:
                send_part(mine, q).wait_send()


def body(core_ids, bag_lengths, first_core, middle_core, last_core, grad_hidden):
    nd, nt = lax.axis_size("dp"), lax.axis_size("table")
    block, hidden = grad_hidden.shape
    ncore = middle_core.shape[1]
    ids = jnp.transpose(core_ids, (1, 2, 3, 0))
    shape = (nt, 3, BAG, block)
    unused = lax.broadcasted_iota(jnp.int32, shape, 2) >= jnp.transpose(bag_lengths)[:, None, None, :]
    ids = jnp.where(jnp.logical_and(unused, lax.broadcasted_iota(jnp.int32, shape, 1) == 0), ncore, ids)
    cols = hidden // nd
    half = hidden // 2
    vmem = pl.BlockSpec(memory_space=pltpu.VMEM)
    hbm = pl.BlockSpec(memory_space=pltpu.HBM)
    dma = pltpu.SemaphoreType.DMA
    padded = ncore // 16 * 16 + 16
    return pl.pallas_call(
        functools.partial(kernel, nd, nt),
        out_shape=(
            jax.ShapeDtypeStruct((block, nt * WIDTH), BF16),
            jax.ShapeDtypeStruct((WIDTH, cols), F32),
        ),
        in_specs=[vmem] + [hbm] * 4,
        out_specs=(vmem, vmem),
        scratch_shapes=[
            pltpu.VMEM((nt, 8, block), jnp.int32),
            pltpu.VMEM((nt, 8, block), jnp.int32),
            pltpu.SMEM((3, 8, block), jnp.int32),
            pltpu.VMEM((ncore, RANK, D2 * RANK), BF16),
            pltpu.VMEM((2, ncore, D1 * RANK), BF16),
            pltpu.VMEM((nt, block, half), BF16),
            pltpu.VMEM((nt, block, WIDTH), BF16),
            pltpu.VMEM((nt, block, WIDTH), BF16),
            pltpu.VMEM((padded, D1, LANES), F32),
            pltpu.VMEM((padded * D2 * D3, LANES), F32),
            pltpu.VMEM((padded, D2 * D3, LANES), BF16),
            pltpu.VMEM((LAG, 8 * D1, BAG * LANES), BF16),
            pltpu.VMEM((block, LANES), F32),
            pltpu.VMEM((block, WIDTH), F32),
            pltpu.VMEM((2, nd // 2, WIDTH, cols), BF16),
            pltpu.VMEM((nd, WIDTH, cols), BF16),
            dma, dma((2,)), dma, dma((3,)),
            dma((nt,)), dma((nt,)), dma((nt,)), dma((nt,)), dma((nt,)), dma((nt,)),
            dma((nt,)), dma((nt,)), dma((2, nd // 2)), dma((nd,)),
        ],
        compiler_params=pltpu.CompilerParams(
            collective_id=0, has_side_effects=True, vmem_limit_bytes=54784 * 1024
        ),
        cost_estimate=pl.CostEstimate(flops=2 * 10**9, bytes_accessed=6 * 10**6, transcendentals=0),
    )(ids, first_core[0], middle_core[0], last_core[0], grad_hidden)


def solution(mesh):
    placed = (
        P(("dp", "table"), None, None, None),
        P(("dp", "table"), None),
        P("table", None, None),
        P("table", None, None, None),
        P("table", None, None),
        P(("dp", "table"), None),
    )
    return jax.shard_map(
        body,
        mesh=mesh,
        in_specs=placed,
        out_specs=(P(("dp", "table"), None), P("table", "dp")),
        check_vma=False,
    )
```

```python
import functools

import jax
import jax.numpy as jnp
from jax import lax
from jax.experimental import pallas as pl
from jax.experimental.pallas import tpu as pltpu
from jax.sharding import PartitionSpec as P

D1 = 8
D2 = 2
D3 = 8
RANK = 64
BAG = 2
LANES = 128
WIDTH = D1 * D2 * D3
SPAN = D1 * LANES
LAG = 2
MESH = pl.DeviceIdType.MESH
F32 = jnp.float32
BF16 = jnp.bfloat16


def iota(shape, dim):
    return lax.broadcasted_iota(jnp.int32, shape, dim)


def spread_tables(first, last, firstx, wide, lastx):
    ncore, length = first.shape
    wide[0 : firstx.shape[0] * D1] = jnp.zeros((firstx.shape[0] * D1, LANES), F32)
    lower = iota((ncore, LANES), 1) < RANK
    for a in range(0, D1, 2):
        both = first[:, a * RANK : (a + 2) * RANK].astype(F32)
        turned = pltpu.roll(both, RANK, 1)
        wide[pl.ds(a, ncore, stride=D1), :] = jnp.where(lower, both, turned)
        wide[pl.ds(a + 1, ncore, stride=D1), :] = jnp.where(lower, turned, both)
    firstx[...] = wide[0 : firstx.shape[0] * D1].reshape(firstx.shape)
    row, lane = iota((length, 2 * LANES), 0), iota((length, 2 * LANES), 1)
    want = row - lax.rem(lane, RANK) * D3 - lane // LANES
    for c in range(0, D3, 2):
        pick = (want == c).astype(F32).astype(BF16)
        found = jnp.dot(last[...], pick, preferred_element_type=F32)
        for e in range(2):
            one = found[:, e * LANES : (e + 1) * LANES]
            wide[pl.ds(c + e, ncore, stride=D2 * D3), :] = jnp.where(lower, one, 0.0)
            wide[pl.ds(D3 + c + e, ncore, stride=D2 * D3), :] = jnp.where(lower, 0.0, one)
    lastx[...] = wide[...].reshape(lastx.shape).astype(BF16)


def heads_of(smem, slot, firstx, middle, at):
    upper = (iota((8, LANES), 1) >= RANK).astype(F32)
    lower = 1.0 - upper
    zero = jnp.zeros((16, LANES), BF16)
    groups = []
    for g in range(2):
        lefts, rights = [], []
        for j in range(BAG):
            heads, centres = [], []
            for i in range(4):
                n = at + g * 4 + i
                heads.append(firstx[smem[slot, j, n]] * (upper if i % 2 else lower))
                centres.append(middle[smem[slot, 2 + j, n]])
            top = jnp.concatenate(heads[:2], axis=0).astype(BF16)
            low = jnp.concatenate(heads[2:], axis=0).astype(BF16)
            lefts.append(jnp.concatenate([top, zero], axis=1))
            lefts.append(jnp.concatenate([zero, low], axis=1))
            rights.append(jnp.concatenate(centres, axis=0))
        both = jnp.dot(jnp.concatenate(lefts, axis=0), jnp.concatenate(rights, axis=1),
                       preferred_element_type=F32)
        groups.append(jnp.concatenate(
            [both[j * 32 : (j + 1) * 32, j * LANES : (j + 1) * LANES] for j in range(BAG)], axis=1
        ).astype(BF16))
    return jnp.concatenate(groups, axis=0)


def tails_of(smem, slot, prefix, lastx, at):
    sides = []
    for j in range(BAG):
        tails = []
        for i in range(8):
            tails.append(lastx[smem[slot, 4 + j, at + i]])
        sides.append(jnp.concatenate(tails, axis=0))
    out = lax.dot_general(prefix, jnp.concatenate(sides, axis=1), (((1,), (1,)), ((), ())),
                          preferred_element_type=F32)
    owner = iota((8, LANES), 1) // 16
    total = out[0:8]
    for i in range(1, 8):
        total = jnp.where(owner == i, out[i * 8 : (i + 1) * 8], total)
    return total


def finish(smem, slot, lastx, kept, found, block):
    for e in range(LAG):
        h = block // 8 - LAG + e
        found[h * 8 : (h + 1) * 8, :] = tails_of(smem, slot, kept[e], lastx, h * 8)


def lookups(smem, slot, old, firstx, middle, lastx, kept, found, ordered, block):
    count = block // 8
    prefixes = {g: heads_of(smem, slot, firstx, middle, g * 8) for g in range(LAG)}
    finish(smem, old, lastx, kept, found, block)
    before = found[...].astype(BF16)
    for g in range(LAG, count):
        prefixes[g] = heads_of(smem, slot, firstx, middle, g * 8)
        h = g - LAG
        found[h * 8 : (h + 1) * 8, :] = tails_of(smem, slot, prefixes.pop(h), lastx, h * 8)
        if g == 2 * LAG:
            done = unfold(before, ordered, block)
    for e in range(LAG):
        kept[e] = prefixes.pop(count - LAG + e)
    return done


def unfold(values, ordered, block):
    count = block // 8
    row, col = iota((LANES, SPAN), 0), iota((LANES, SPAN), 1)
    copies = jnp.logical_and(row // 16 == col // LANES, lax.rem(row, 16) == lax.rem(col, 16))
    copied = jnp.dot(values, copies.astype(F32).astype(BF16), preferred_element_type=F32)
    row, col = iota((block, LANES), 0), iota((block, LANES), 1)
    keep = (lax.rem(row, 8) == col // 16).astype(F32)
    kept = jnp.concatenate(
        [copied[:, i * LANES : (i + 1) * LANES] * keep for i in range(8)], axis=1).astype(BF16)
    add = (iota((count, block), 1) // 8 == iota((count, block), 0)).astype(F32).astype(BF16)
    sums = jnp.dot(add, kept, preferred_element_type=F32)
    for i in range(8):
        ordered[pl.ds(i, count, stride=8), :] = sums[:, i * LANES : (i + 1) * LANES]
    return ordered[...].astype(BF16)


def kernel(nd, nt, raw_ids, first, middle, last, grad, pooled, wg,
           tiles, ids, smem, mid, ends, grads, rows, sib, firstx, wide, lastx, kept, found, ordered, part, partin,
           mid_sem, end_sem, own_sem, smem_sem, ids_ss, ids_rs, grad_ss, grad_rs, pool_ss, pool_rs, sib_ss, sib_rs,
           part_ss, part_rs):
    d, t = lax.axis_index("dp"), lax.axis_index("table")
    core = lax.rem(t, 2)
    pair = t - core
    other = pair + 1 - core
    block = grad.shape[0]
    half = grads.shape[2]
    cols = wg.shape[1]
    per = nd // 2

    load = pltpu.make_async_copy(middle, mid, mid_sem)
    loads = [pltpu.make_async_copy(ref, ends.at[k], end_sem.at[k]) for k, ref in enumerate((first, last))]
    for copy in loads:
        copy.start()
    load.start()

    barrier = pltpu.get_barrier_semaphore()
    for k in range(1, nt):
        pl.semaphore_signal(barrier, inc=1, device_id=(d, lax.rem(t + k, nt)), device_id_type=MESH)
    for k in range(1, nd):
        for e in range(2):
            pl.semaphore_signal(
                barrier, inc=1, device_id=(lax.rem(d + k, nd), pair + e), device_id_type=MESH
            )
    own = pltpu.make_async_copy(
        grad.at[:, pl.ds(pl.multiple_of(core * half, LANES), half)], grads.at[t], own_sem)
    own.start()
    for k in range(nt):
        tiles[k, 0:BAG] = raw_ids[k, 0]
        tiles[k, BAG : 2 * BAG] = raw_ids[k, 1]
        tiles[k, 2 * BAG : 3 * BAG] = raw_ids[k, 2]
        tiles[k, 3 * BAG :] = jnp.zeros((8 - 3 * BAG, block), jnp.int32)
    pltpu.make_async_copy(tiles.at[t], smem.at[0], smem_sem.at[0]).start()
    blank = pltpu.make_async_copy(tiles.at[t], smem.at[2], smem_sem.at[2])
    blank.start()
    kept[...] = jnp.zeros_like(kept)
    found[...] = jnp.zeros_like(found)
    pl.semaphore_wait(barrier, nt - 1 + 2 * (nd - 1))

    def send_ids(k):
        peer = lax.rem(t + k, nt)
        return pltpu.make_async_remote_copy(
            tiles.at[peer], ids.at[t], ids_ss.at[k], ids_rs.at[k],
            device_id=(d, peer), device_id_type=MESH)

    def send_grad(k):
        peer = lax.rem(t + k, nt)
        mine = pl.ds(pl.multiple_of(lax.rem(peer, 2) * half, LANES), half)
        return pltpu.make_async_remote_copy(
            grad.at[:, mine], grads.at[t], grad_ss.at[k], grad_rs.at[k],
            device_id=(d, peer), device_id_type=MESH)

    def send_pooled(k):
        peer = lax.rem(t - k + nt, nt)
        return pltpu.make_async_remote_copy(
            rows.at[peer], pooled.at[:, pl.ds(pl.multiple_of(t * WIDTH, LANES), WIDTH)],
            pool_ss.at[k], pool_rs.at[k], device_id=(d, peer), device_id_type=MESH)

    def send_sib(k):
        peer = lax.rem(t - k + nt, nt)
        return pltpu.make_async_remote_copy(
            rows.at[peer], sib.at[peer], sib_ss.at[peer], sib_rs.at[peer],
            device_id=(d, other), device_id_type=MESH)

    for k in range(1, nt):
        send_ids(k).start()
    for k in range(1, nt):
        send_grad(k).start()
    for copy in loads:
        copy.wait()
    spread_tables(ends.at[0], ends.at[1], firstx, wide, lastx)
    load.wait()
    blank.wait()

    def chunk(k, carry):
        s = lax.rem(t - k + nt, nt)
        slot, after_slot, old = lax.rem(k, 3), lax.rem(k + 1, 3), lax.rem(k + 2, 3)
        pltpu.make_async_copy(ids.at[s], smem.at[slot], smem_sem.at[slot]).wait()

        @pl.when(k + 1 < nt)
        def _():
            after = lax.rem(t - k - 1 + nt, nt)
            pltpu.make_async_remote_copy(
                ids.at[after], ids.at[after], ids_ss.at[k + 1], ids_rs.at[k + 1],
                device_id=(d, other), device_id_type=MESH).wait_recv()
            pltpu.make_async_copy(ids.at[after], smem.at[after_slot], smem_sem.at[after_slot]).start()

        rows[lax.rem(s + 1, nt)] = lookups(
            smem, slot, old, firstx, mid, lastx, kept, found, ordered, block)

        @pl.when(k > 0)
        def _():
            send_sib(k - 1).start()

        @pl.when(k > 1)
        def _():
            send_pooled(k - 1).start()

        return carry

    lax.fori_loop(0, nt, chunk, 0)
    own.wait()

    for k in range(1, nt):
        s = lax.rem(t - k + nt, nt)
        pltpu.make_async_remote_copy(
            grads.at[s], grads.at[s], grad_ss.at[k], grad_rs.at[k],
            device_id=(d, other), device_id_type=MESH).wait_recv()
    group = nt * block
    final = lax.rem(t + 1, nt)

    def early(left):
        return lax.dot_general(
            left[...].reshape(group, WIDTH), grads[...].reshape(group, half),
            (((0,), (0,)), ((), ())), preferred_element_type=F32)

    sums = early(rows)
    finish(smem, lax.rem(nt - 1, 3), lastx, kept, found, block)
    rows[lax.rem(t + 1, nt)] = unfold(found[...].astype(BF16), ordered, block)
    send_sib(nt - 1).start()
    send_pooled(nt - 1).start()
    pooled[:, pl.ds(pl.multiple_of(t * WIDTH, LANES), WIDTH)] = rows[t]

    def partial(mine):
        if not mine:
            return early(sib).astype(BF16)
        more = lax.dot_general(
            rows[final], grads[final], (((0,), (0,)), ((), ())), preferred_element_type=F32)
        return (sums + more).astype(BF16)

    def send_part(mine, q):
        target = core * per + q
        return pltpu.make_async_remote_copy(
            part.at[mine, q], partin.at[d], part_ss.at[mine, q], part_rs.at[d],
            device_id=(target, t if mine else other), device_id_type=MESH)

    for mine in (1, 0):
        if not mine:
            for s in range(nt):
                pltpu.make_async_remote_copy(
                    sib.at[s], sib.at[s], sib_ss.at[s], sib_rs.at[s],
                    device_id=(d, other), device_id_type=MESH).wait_recv()
        whole = partial(mine)
        for q in range(per):
            part[mine, q] = whole[:, q * cols : (q + 1) * cols]
            if mine:
                @pl.when(core * per + q != d)
                def _():
                    send_part(mine, q).start()

                @pl.when(core * per + q == d)
                def _():
                    partin[d] = part[mine, q]
            else:
                send_part(mine, q).start()

    for k in range(1, nt):
        send_ids(k).wait_send()
        send_grad(k).wait_send()
        send_pooled(k).wait_send()
        s = lax.rem(t + k, nt)
        pltpu.make_async_remote_copy(
            rows.at[s], pooled.at[:, pl.ds(pl.multiple_of(s * WIDTH, LANES), WIDTH)],
            pool_ss.at[k], pool_rs.at[k], device_id=(d, other), device_id_type=MESH).wait_recv()
    for k in range(nt):
        send_sib(k).wait_send()

    source = d // per
    for k in range(nd):
        @pl.when(jnp.logical_or(source != core, k != d))
        def _():
            pltpu.make_async_remote_copy(
                partin.at[k], partin.at[k], part_ss.at[0, 0], part_rs.at[k],
                device_id=(d, other), device_id_type=MESH).wait_recv()
    total = partin[0].astype(F32)
    for k in range(1, nd):
        total = total + partin[k].astype(F32)
    wg[...] = total
    for mine in (1, 0):
        for q in range(per):
            if mine:
                @pl.when(core * per + q != d)
                def _():
                    send_part(mine, q).wait_send()
            else:
                send_part(mine, q).wait_send()


def body(core_ids, bag_lengths, first_core, middle_core, last_core, grad_hidden):
    nd, nt = lax.axis_size("dp"), lax.axis_size("table")
    block, hidden = grad_hidden.shape
    ncore = middle_core.shape[1]
    ids = jnp.transpose(core_ids, (1, 2, 3, 0))
    shape = (nt, 3, BAG, block)
    unused = lax.broadcasted_iota(jnp.int32, shape, 2) >= jnp.transpose(bag_lengths)[:, None, None, :]
    ids = jnp.where(jnp.logical_and(unused, lax.broadcasted_iota(jnp.int32, shape, 1) == 0), ncore, ids)
    cols = hidden // nd
    half = hidden // 2
    vmem = pl.BlockSpec(memory_space=pltpu.VMEM)
    hbm = pl.BlockSpec(memory_space=pltpu.HBM)
    dma = pltpu.SemaphoreType.DMA
    padded = ncore // 16 * 16 + 16
    return pl.pallas_call(
        functools.partial(kernel, nd, nt),
        out_shape=(
            jax.ShapeDtypeStruct((block, nt * WIDTH), BF16),
            jax.ShapeDtypeStruct((WIDTH, cols), F32),
        ),
        in_specs=[vmem] + [hbm] * 4,
        out_specs=(vmem, vmem),
        scratch_shapes=[
            pltpu.VMEM((nt, 8, block), jnp.int32),
            pltpu.VMEM((nt, 8, block), jnp.int32),
            pltpu.SMEM((3, 8, block), jnp.int32),
            pltpu.VMEM((ncore, RANK, D2 * RANK), BF16),
            pltpu.VMEM((2, ncore, D1 * RANK), BF16),
            pltpu.VMEM((nt, block, half), BF16),
            pltpu.VMEM((nt, block, WIDTH), BF16),
            pltpu.VMEM((nt, block, WIDTH), BF16),
            pltpu.VMEM((padded, D1, LANES), F32),
            pltpu.VMEM((padded * D2 * D3, LANES), F32),
            pltpu.VMEM((padded, D2 * D3, LANES), BF16),
            pltpu.VMEM((LAG, 8 * D1, BAG * LANES), BF16),
            pltpu.VMEM((block, LANES), F32),
            pltpu.VMEM((block, WIDTH), F32),
            pltpu.VMEM((2, nd // 2, WIDTH, cols), BF16),
            pltpu.VMEM((nd, WIDTH, cols), BF16),
            dma, dma((2,)), dma, dma((3,)),
            dma((nt,)), dma((nt,)), dma((nt,)), dma((nt,)), dma((nt,)), dma((nt,)),
            dma((nt,)), dma((nt,)), dma((2, nd // 2)), dma((nd,)),
        ],
        compiler_params=pltpu.CompilerParams(
            collective_id=0, has_side_effects=True, vmem_limit_bytes=54784 * 1024
        ),
        cost_estimate=pl.CostEstimate(flops=2 * 10**9, bytes_accessed=6 * 10**6, transcendentals=0),
    )(ids, first_core[0], middle_core[0], last_core[0], grad_hidden)


def solution(mesh):
    placed = (
        P(("dp", "table"), None, None, None),
        P(("dp", "table"), None),
        P("table", None, None),
        P("table", None, None, None),
        P("table", None, None),
        P(("dp", "table"), None),
    )
    return jax.shard_map(
        body,
        mesh=mesh,
        in_specs=placed,
        out_specs=(P(("dp", "table"), None), P("table", "dp")),
        check_vma=False,
    )
```

```python
import functools

import jax
import jax.numpy as jnp
from jax import lax
from jax.experimental import pallas as pl
from jax.experimental.pallas import tpu as pltpu
from jax.sharding import PartitionSpec as P

D1 = 8
D2 = 2
D3 = 8
RANK = 64
BAG = 2
LANES = 128
WIDTH = D1 * D2 * D3
SPAN = D1 * LANES
LAG = 2
MESH = pl.DeviceIdType.MESH
F32 = jnp.float32
BF16 = jnp.bfloat16


def iota(shape, dim):
    return lax.broadcasted_iota(jnp.int32, shape, dim)


def spread_tables(first, last, firstx, wide, lastx):
    ncore, length = first.shape
    wide[0 : firstx.shape[0] * D1] = jnp.zeros((firstx.shape[0] * D1, LANES), F32)
    lower = iota((ncore, LANES), 1) < RANK
    for a in range(0, D1, 2):
        both = first[:, a * RANK : (a + 2) * RANK].astype(F32)
        turned = pltpu.roll(both, RANK, 1)
        wide[pl.ds(a, ncore, stride=D1), :] = jnp.where(lower, both, turned)
        wide[pl.ds(a + 1, ncore, stride=D1), :] = jnp.where(lower, turned, both)
    firstx[...] = wide[0 : firstx.shape[0] * D1].reshape(firstx.shape)
    row, lane = iota((length, 2 * LANES), 0), iota((length, 2 * LANES), 1)
    want = row - lax.rem(lane, RANK) * D3 - lane // LANES
    for c in range(0, D3, 2):
        pick = (want == c).astype(F32).astype(BF16)
        found = jnp.dot(last[...], pick, preferred_element_type=F32)
        for e in range(2):
            one = found[:, e * LANES : (e + 1) * LANES]
            wide[pl.ds(c + e, ncore, stride=D2 * D3), :] = jnp.where(lower, one, 0.0)
            wide[pl.ds(D3 + c + e, ncore, stride=D2 * D3), :] = jnp.where(lower, 0.0, one)
    lastx[...] = wide[...].reshape(lastx.shape).astype(BF16)


def heads_of(smem, slot, firstx, middle, at):
    upper = (iota((8, LANES), 1) >= RANK).astype(F32)
    lower = 1.0 - upper
    zero = jnp.zeros((16, LANES), BF16)
    groups = []
    for g in range(2):
        slots = []
        for j in range(BAG):
            heads, centres = [], []
            for i in range(4):
                n = at + g * 4 + i
                heads.append(firstx[smem[slot, j, n]] * (upper if i % 2 else lower))
                centres.append(middle[smem[slot, 2 + j, n]])
            top = jnp.concatenate(heads[:2], axis=0).astype(BF16)
            low = jnp.concatenate(heads[2:], axis=0).astype(BF16)
            left = jnp.concatenate(
                [jnp.concatenate([top, zero], axis=1), jnp.concatenate([zero, low], axis=1)], axis=0)
            slots.append(jnp.dot(left, jnp.concatenate(centres, axis=0), preferred_element_type=F32))
        groups.append(jnp.concatenate(slots, axis=1).astype(BF16))
    return jnp.concatenate(groups, axis=0)


def tails_of(smem, slot, prefix, lastx, at):
    sides = []
    for j in range(BAG):
        tails = []
        for i in range(8):
            tails.append(lastx[smem[slot, 4 + j, at + i]])
        sides.append(jnp.concatenate(tails, axis=0))
    out = lax.dot_general(prefix, jnp.concatenate(sides, axis=1), (((1,), (1,)), ((), ())),
                          preferred_element_type=F32)
    owner = iota((8, LANES), 1) // 16
    total = out[0:8]
    for i in range(1, 8):
        total = jnp.where(owner == i, out[i * 8 : (i + 1) * 8], total)
    return total


def finish(smem, slot, lastx, kept, found, block):
    for e in range(LAG):
        h = block // 8 - LAG + e
        found[h * 8 : (h + 1) * 8, :] = tails_of(smem, slot, kept[e], lastx, h * 8)


def lookups(smem, slot, old, firstx, middle, lastx, kept, found, ordered, block):
    count = block // 8
    prefixes = {g: heads_of(smem, slot, firstx, middle, g * 8) for g in range(LAG)}
    finish(smem, old, lastx, kept, found, block)
    before = found[...].astype(BF16)
    for g in range(LAG, count):
        prefixes[g] = heads_of(smem, slot, firstx, middle, g * 8)
        h = g - LAG
        found[h * 8 : (h + 1) * 8, :] = tails_of(smem, slot, prefixes.pop(h), lastx, h * 8)
        if g == 2 * LAG:
            done = unfold(before, ordered, block)
    for e in range(LAG):
        kept[e] = prefixes.pop(count - LAG + e)
    return done


def unfold(values, ordered, block):
    count = block // 8
    row, col = iota((LANES, SPAN), 0), iota((LANES, SPAN), 1)
    copies = jnp.logical_and(row // 16 == col // LANES, lax.rem(row, 16) == lax.rem(col, 16))
    copied = jnp.dot(values, copies.astype(F32).astype(BF16), preferred_element_type=F32)
    row, col = iota((block, LANES), 0), iota((block, LANES), 1)
    keep = (lax.rem(row, 8) == col // 16).astype(F32)
    kept = jnp.concatenate(
        [copied[:, i * LANES : (i + 1) * LANES] * keep for i in range(8)], axis=1).astype(BF16)
    add = (iota((count, block), 1) // 8 == iota((count, block), 0)).astype(F32).astype(BF16)
    sums = jnp.dot(add, kept, preferred_element_type=F32)
    for i in range(8):
        ordered[pl.ds(i, count, stride=8), :] = sums[:, i * LANES : (i + 1) * LANES]
    return ordered[...].astype(BF16)


def kernel(nd, nt, raw_ids, first, middle, last, grad, pooled, wg,
           tiles, ids, smem, mid, ends, grads, rows, sib, firstx, wide, lastx, kept, found, ordered, part, partin,
           mid_sem, end_sem, own_sem, smem_sem, ids_ss, ids_rs, grad_ss, grad_rs, pool_ss, pool_rs, sib_ss, sib_rs,
           part_ss, part_rs):
    d, t = lax.axis_index("dp"), lax.axis_index("table")
    core = lax.rem(t, 2)
    pair = t - core
    other = pair + 1 - core
    block = grad.shape[0]
    half = grads.shape[2]
    cols = wg.shape[1]
    per = nd // 2

    load = pltpu.make_async_copy(middle, mid, mid_sem)
    loads = [pltpu.make_async_copy(ref, ends.at[k], end_sem.at[k]) for k, ref in enumerate((first, last))]
    for copy in loads:
        copy.start()
    load.start()

    barrier = pltpu.get_barrier_semaphore()
    for k in range(1, nt):
        pl.semaphore_signal(barrier, inc=1, device_id=(d, lax.rem(t + k, nt)), device_id_type=MESH)
    for k in range(1, nd):
        for e in range(2):
            pl.semaphore_signal(
                barrier, inc=1, device_id=(lax.rem(d + k, nd), pair + e), device_id_type=MESH
            )
    own = pltpu.make_async_copy(
        grad.at[:, pl.ds(pl.multiple_of(core * half, LANES), half)], grads.at[t], own_sem)
    own.start()
    for k in range(nt):
        tiles[k, 0:BAG] = raw_ids[k, 0]
        tiles[k, BAG : 2 * BAG] = raw_ids[k, 1]
        tiles[k, 2 * BAG : 3 * BAG] = raw_ids[k, 2]
        tiles[k, 3 * BAG :] = jnp.zeros((8 - 3 * BAG, block), jnp.int32)
    pltpu.make_async_copy(tiles.at[t], smem.at[0], smem_sem.at[0]).start()
    blank = pltpu.make_async_copy(tiles.at[t], smem.at[2], smem_sem.at[2])
    blank.start()
    kept[...] = jnp.zeros_like(kept)
    found[...] = jnp.zeros_like(found)
    pl.semaphore_wait(barrier, nt - 1 + 2 * (nd - 1))

    def send_ids(k):
        peer = lax.rem(t + k, nt)
        return pltpu.make_async_remote_copy(
            tiles.at[peer], ids.at[t], ids_ss.at[k], ids_rs.at[k],
            device_id=(d, peer), device_id_type=MESH)

    def send_grad(k):
        peer = lax.rem(t + k, nt)
        mine = pl.ds(pl.multiple_of(lax.rem(peer, 2) * half, LANES), half)
        return pltpu.make_async_remote_copy(
            grad.at[:, mine], grads.at[t], grad_ss.at[k], grad_rs.at[k],
            device_id=(d, peer), device_id_type=MESH)

    def send_pooled(k):
        peer = lax.rem(t - k + nt, nt)
        return pltpu.make_async_remote_copy(
            rows.at[peer], pooled.at[:, pl.ds(pl.multiple_of(t * WIDTH, LANES), WIDTH)],
            pool_ss.at[k], pool_rs.at[k], device_id=(d, peer), device_id_type=MESH)

    def send_sib(k):
        peer = lax.rem(t - k + nt, nt)
        return pltpu.make_async_remote_copy(
            rows.at[peer], sib.at[peer], sib_ss.at[peer], sib_rs.at[peer],
            device_id=(d, other), device_id_type=MESH)

    for k in range(1, nt):
        send_ids(k).start()
    for k in range(1, nt):
        send_grad(k).start()
    for copy in loads:
        copy.wait()
    spread_tables(ends.at[0], ends.at[1], firstx, wide, lastx)
    load.wait()
    blank.wait()

    def chunk(k, carry):
        s = lax.rem(t - k + nt, nt)
        slot, after_slot, old = lax.rem(k, 3), lax.rem(k + 1, 3), lax.rem(k + 2, 3)
        pltpu.make_async_copy(ids.at[s], smem.at[slot], smem_sem.at[slot]).wait()

        @pl.when(k + 1 < nt)
        def _():
            after = lax.rem(t - k - 1 + nt, nt)
            pltpu.make_async_remote_copy(
                ids.at[after], ids.at[after], ids_ss.at[k + 1], ids_rs.at[k + 1],
                device_id=(d, other), device_id_type=MESH).wait_recv()
            pltpu.make_async_copy(ids.at[after], smem.at[after_slot], smem_sem.at[after_slot]).start()

        rows[lax.rem(s + 1, nt)] = lookups(
            smem, slot, old, firstx, mid, lastx, kept, found, ordered, block)

        @pl.when(k > 0)
        def _():
            send_sib(k - 1).start()

        @pl.when(k > 1)
        def _():
            send_pooled(k - 1).start()

        return carry

    lax.fori_loop(0, nt, chunk, 0)
    finish(smem, lax.rem(nt - 1, 3), lastx, kept, found, block)
    rows[lax.rem(t + 1, nt)] = unfold(found[...].astype(BF16), ordered, block)
    send_sib(nt - 1).start()
    send_pooled(nt - 1).start()
    pooled[:, pl.ds(pl.multiple_of(t * WIDTH, LANES), WIDTH)] = rows[t]
    own.wait()

    for k in range(1, nt):
        s = lax.rem(t - k + nt, nt)
        pltpu.make_async_remote_copy(
            grads.at[s], grads.at[s], grad_ss.at[k], grad_rs.at[k],
            device_id=(d, other), device_id_type=MESH).wait_recv()
    group = nt * block

    def partial(mine):
        left = rows if mine else sib
        return lax.dot_general(
            left[...].reshape(group, WIDTH), grads[...].reshape(group, half),
            (((0,), (0,)), ((), ())), preferred_element_type=F32).astype(BF16)

    def send_part(mine, q):
        target = core * per + q
        return pltpu.make_async_remote_copy(
            part.at[mine, q], partin.at[d], part_ss.at[mine, q], part_rs.at[d],
            device_id=(target, t if mine else other), device_id_type=MESH)

    for mine in (1, 0):
        if not mine:
            for s in range(nt):
                pltpu.make_async_remote_copy(
                    sib.at[s], sib.at[s], sib_ss.at[s], sib_rs.at[s],
                    device_id=(d, other), device_id_type=MESH).wait_recv()
        whole = partial(mine)
        for q in range(per):
            part[mine, q] = whole[:, q * cols : (q + 1) * cols]
            if mine:
                @pl.when(core * per + q != d)
                def _():
                    send_part(mine, q).start()

                @pl.when(core * per + q == d)
                def _():
                    partin[d] = part[mine, q]
            else:
                send_part(mine, q).start()

    for k in range(1, nt):
        send_ids(k).wait_send()
        send_grad(k).wait_send()
        send_pooled(k).wait_send()
        s = lax.rem(t + k, nt)
        pltpu.make_async_remote_copy(
            rows.at[s], pooled.at[:, pl.ds(pl.multiple_of(s * WIDTH, LANES), WIDTH)],
            pool_ss.at[k], pool_rs.at[k], device_id=(d, other), device_id_type=MESH).wait_recv()
    for k in range(nt):
        send_sib(k).wait_send()

    source = d // per
    for k in range(nd):
        @pl.when(jnp.logical_or(source != core, k != d))
        def _():
            pltpu.make_async_remote_copy(
                partin.at[k], partin.at[k], part_ss.at[0, 0], part_rs.at[k],
                device_id=(d, other), device_id_type=MESH).wait_recv()
    total = partin[0].astype(F32)
    for k in range(1, nd):
        total = total + partin[k].astype(F32)
    wg[...] = total
    for mine in (1, 0):
        for q in range(per):
            if mine:
                @pl.when(core * per + q != d)
                def _():
                    send_part(mine, q).wait_send()
            else:
                send_part(mine, q).wait_send()


def body(core_ids, bag_lengths, first_core, middle_core, last_core, grad_hidden):
    nd, nt = lax.axis_size("dp"), lax.axis_size("table")
    block, hidden = grad_hidden.shape
    ncore = middle_core.shape[1]
    ids = jnp.transpose(core_ids, (1, 2, 3, 0))
    shape = (nt, 3, BAG, block)
    unused = lax.broadcasted_iota(jnp.int32, shape, 2) >= jnp.transpose(bag_lengths)[:, None, None, :]
    ids = jnp.where(jnp.logical_and(unused, lax.broadcasted_iota(jnp.int32, shape, 1) == 0), ncore, ids)
    cols = hidden // nd
    half = hidden // 2
    vmem = pl.BlockSpec(memory_space=pltpu.VMEM)
    hbm = pl.BlockSpec(memory_space=pltpu.HBM)
    dma = pltpu.SemaphoreType.DMA
    padded = ncore // 16 * 16 + 16
    return pl.pallas_call(
        functools.partial(kernel, nd, nt),
        out_shape=(
            jax.ShapeDtypeStruct((block, nt * WIDTH), BF16),
            jax.ShapeDtypeStruct((WIDTH, cols), F32),
        ),
        in_specs=[vmem] + [hbm] * 4,
        out_specs=(vmem, vmem),
        scratch_shapes=[
            pltpu.VMEM((nt, 8, block), jnp.int32),
            pltpu.VMEM((nt, 8, block), jnp.int32),
            pltpu.SMEM((3, 8, block), jnp.int32),
            pltpu.VMEM((ncore, RANK, D2 * RANK), BF16),
            pltpu.VMEM((2, ncore, D1 * RANK), BF16),
            pltpu.VMEM((nt, block, half), BF16),
            pltpu.VMEM((nt, block, WIDTH), BF16),
            pltpu.VMEM((nt, block, WIDTH), BF16),
            pltpu.VMEM((padded, D1, LANES), F32),
            pltpu.VMEM((padded * D2 * D3, LANES), F32),
            pltpu.VMEM((padded, D2 * D3, LANES), BF16),
            pltpu.VMEM((LAG, 8 * D1, BAG * LANES), BF16),
            pltpu.VMEM((block, LANES), F32),
            pltpu.VMEM((block, WIDTH), F32),
            pltpu.VMEM((2, nd // 2, WIDTH, cols), BF16),
            pltpu.VMEM((nd, WIDTH, cols), BF16),
            dma, dma((2,)), dma, dma((3,)),
            dma((nt,)), dma((nt,)), dma((nt,)), dma((nt,)), dma((nt,)), dma((nt,)),
            dma((nt,)), dma((nt,)), dma((2, nd // 2)), dma((nd,)),
        ],
        compiler_params=pltpu.CompilerParams(
            collective_id=0, has_side_effects=True, vmem_limit_bytes=54784 * 1024
        ),
        cost_estimate=pl.CostEstimate(flops=2 * 10**9, bytes_accessed=6 * 10**6, transcendentals=0),
    )(ids, first_core[0], middle_core[0], last_core[0], grad_hidden)


def solution(mesh):
    placed = (
        P(("dp", "table"), None, None, None),
        P(("dp", "table"), None),
        P("table", None, None),
        P("table", None, None, None),
        P("table", None, None),
        P(("dp", "table"), None),
    )
    return jax.shard_map(
        body,
        mesh=mesh,
        in_specs=placed,
        out_specs=(P(("dp", "table"), None), P("table", "dp")),
        check_vma=False,
    )
```
